512 devices in a mesh: row: 64 (over y_lo, z, core), col: 8 (over x, y_hi).
Axes of the slice: x: 4, y: 4 (y_hi: 2, y_lo: 2; y = y_hi * 2 + y_lo), z: 16, core: 2. Of those that a mesh axis runs over, the one named last changes fastest.
Arguments:
- sensitivity: float32 [16384, 16384], P('row', 'col'), as said below
- injections: bfloat16 [16384, 2048], P('col', 'row'), may hold values from -6 to 6
- from_node: int32 [64], replicated, may hold values from 0 to 16383, as said below
- to_node: int32 [64], replicated, may hold values from 1 to 16382, as said below
- switch_flags: int32 [64], replicated, may hold values 0 or 1
- impedance: float32 [64], replicated, may hold values from 0.5 to 2
Outputs:
- voltages: float32 [16384, 2048], P('row', 'col')
The draws below stay inside these ranges and needn't reach their ends.
Inputs may be any that keep to these rules, and one draw needn't show every extreme that they name: from_node and to_node together hold 128 distinct nodes; from_node holds nodes 0 and 16383. to_node holds no node of from_node, and no node twice; it holds nodes 1 and 16382. sensitivity is symmetric with diagonal entries of 0.5 to 1.5.
All inputs are finite; a program needn't handle non-finite values.
Results may differ from the reference program's by a relative error of at most 0.0008.
Values may be sent and summed in bfloat16 or wider, within the bound.
No kernel may reach another device: no remote copies, remote signals or barrier semaphores. Data moves between devices by JAX's collectives and lax.ppermute only.
A program may use at most 64 MiB of HBM per device.

```python
import math
import jax
import jax.numpy as jnp
from jax import lax

N = 16384
BR = 64
SLOTS = 2048


def endpoints(key):
    first, second, third = jax.random.split(key, 3)
    inner = (jax.random.permutation(first, N - 4)[:2 * BR - 4] + 2).astype(jnp.int32)
    heads = jnp.concatenate([jnp.array([0, N - 1], jnp.int32), inner[:BR - 2]])
    tails = jnp.concatenate([jnp.array([1, N - 2], jnp.int32), inner[BR - 2:]])
    heads = heads[jax.random.permutation(second, BR)]
    tails = tails[jax.random.permutation(third, BR)]
    return (heads, tails)


def draw_from_node(key, part):
    return endpoints(key)[0]


def draw_to_node(key, part):
    return endpoints(key)[1]


def draw_sensitivity(key, part):
    key = jax.random.fold_in(key, 7)
    first, second = jax.random.split(key)
    spread = 0.28 / math.sqrt(N)
    noise = jax.random.uniform(first, (N, N), jnp.float32, -spread, spread)
    diagonal = jax.random.uniform(second, (N,), jnp.float32, 0.5, 1.5)
    index_rows = jnp.arange(N)[:, None]
    index_cols = jnp.arange(N)[None, :]
    return jnp.where(index_rows == index_cols, diagonal[:, None], noise + noise.T)


def place_ends(values, own_key, least, top_value):
    shape = values.shape
    index_at = [jax.random.randint(jax.random.fold_in(own_key, axis), (), 0, shape[axis]) for axis in range(len(shape))]
    values = values.at[tuple(index_at)].set(least)
    longest = shape.index(max(shape))
    index_at[longest] = (index_at[longest] + 1) % shape[longest]
    return values.at[tuple(index_at)].set(top_value)


def block_levels(stream_key, extent, shards, smallest, high):
    def one(position, blocks):
        draws = jax.random.uniform(jax.random.fold_in(jax.random.fold_in(stream_key, 6), position), (blocks,), jnp.float32, smallest / len(shards), high / len(shards))
        return jnp.repeat(jnp.exp(draws), extent[position] // blocks).reshape((-1,) + (1,) * (len(extent) - position - 1))

    level = one(*shards[0])
    for cut in shards[1:]:
        level = level * one(*cut)
    return level


def normal_values(stream_key, shape, width, most, pieces=(), dtype=jnp.bfloat16):
    result = jax.random.normal(stream_key, shape, jnp.float32) * width
    if len(pieces) > 0:
        result = block_levels(stream_key, shape, pieces, -0.22, 0.18) * result
    return jnp.clip(result, min=-most, max=most).astype(dtype)


def setup_inputs(seed: int = 0) -> dict:
    splits = jax.random.split(jax.random.key(seed), 7)
    return {
        "sensitivity": draw_sensitivity(jax.random.fold_in(splits[6], 71), 0),
        "injections": normal_values(splits[1], (N, SLOTS), 1.0, 6.0, ((0, 8), (1, 64))),
        "from_node": draw_from_node(jax.random.fold_in(splits[6], 71), 0),
        "to_node": draw_to_node(jax.random.fold_in(splits[6], 71), 0),
        "switch_flags": place_ends((jax.random.randint(splits[4], (BR,), 0, 2) < 1).astype(jnp.int32), jax.random.fold_in(splits[4], 1), 0, 1),
        "impedance": jnp.clip(jnp.exp(jax.random.uniform(splits[5], (BR,), jnp.float32, math.log(0.5), math.log(2.0))), 0.5, 2.0),
    }


def incidence_of(node_ids, from_node, to_node):
    plus = (node_ids[:, None] == from_node[None, :]).astype(jnp.float32)
    minus = (node_ids[:, None] == to_node[None, :]).astype(jnp.float32)
    return plus - minus

def reference(sensitivity, injections, from_node, to_node, switch_flags, impedance):
    high = lax.Precision.HIGHEST
    columns = sensitivity[:, from_node] - sensitivity[:, to_node]
    reach = impedance * (1.0 + 3.0 * switch_flags.astype(jnp.float32))
    capacity = columns[from_node] - columns[to_node] + jnp.diag(reach)
    loads = injections.astype(jnp.float32)
    direct = jnp.dot(sensitivity.astype(jnp.float32), loads.astype(jnp.float32), precision=high, preferred_element_type=jnp.float32)
    ends = direct[from_node] - direct[to_node]
    factor = jnp.linalg.cholesky(capacity)
    weights = jax.scipy.linalg.cho_solve((factor, True), ends)
    return direct - jnp.dot(columns.astype(jnp.float32), weights.astype(jnp.float32), precision=high, preferred_element_type=jnp.float32)
```

```python
import jax
import jax.numpy as jnp
from jax import lax
from jax.sharding import PartitionSpec as P

HIGH = lax.Precision.HIGHEST
F32 = jnp.float32
BF16 = jnp.bfloat16

Y, Z, CORES = 2, 16, 2
COLS = 8
BR = 64


def row_of(y, z, core):
    return y * Z * CORES + z * CORES + core


ROWS = [(y, z, core) for y in range(Y) for z in range(Z) for core in range(CORES)]
OTHER_CORE = [(row_of(y, z, k), row_of(y, z, 1 - k)) for y, z, k in ROWS]
OTHER_Y = [(row_of(y, z, k), row_of(1 - y, z, k)) for y, z, k in ROWS]
ALONG_Z = [[row_of(y, z, k) for z in range(Z)] for y in range(Y) for k in range(CORES)]
TO_COLUMN = [
    ((8 * a + b) * COLS + c, (8 * b + c) * COLS + a)
    for a in range(8) for b in range(8) for c in range(8)
]


def incidence_of(node_ids, from_node, to_node):
    plus = (node_ids[:, None] == from_node[None, :]).astype(BF16)
    minus = (node_ids[:, None] == to_node[None, :]).astype(BF16)
    return plus - minus


def split(values):
    high = lax.reduce_precision(values, 8, 7)
    return high.astype(BF16), (values - high).astype(BF16)


def in_order(position, mine, other):
    return jnp.where(position == 0, jnp.stack([mine, other]), jnp.stack([other, mine]))


def nt(left, right):
    return lax.dot_general(left, right, (((1,), (1,)), ((), ())), preferred_element_type=F32)


def on_device(sensitivity, injections, from_node, to_node, switch_flags, impedance):
    row_count, col_count = sensitivity.shape
    row = lax.axis_index("row")
    col = lax.axis_index("col")
    y, core = row // (Z * CORES), row % CORES
    slots = injections.shape[1]

    loads = injections.T
    other_loads = lax.ppermute(loads, "row", OTHER_Y)
    pair = in_order(y, loads, other_loads)
    gathered = lax.all_gather(pair, "row", axis_index_groups=ALONG_Z, axis=0)

    other_rows = lax.ppermute(sensitivity, "row", OTHER_CORE)

    high, low = split(sensitivity)
    col_select = incidence_of(col * col_count + jnp.arange(col_count, dtype=jnp.int32), from_node, to_node)
    row_select = incidence_of(row * row_count + jnp.arange(row_count, dtype=jnp.int32), from_node, to_node)
    part = nt(col_select.T, high) + nt(col_select.T, low)
    parts = lax.all_to_all(jnp.broadcast_to(part[None], (COLS,) + part.shape), "col", 0, 0, tiled=True)
    columns_t = jnp.sum(parts, axis=0)

    width = row_count // COLS
    piece = lax.dynamic_slice_in_dim(columns_t.T, col * width, width, 0)
    piece = jnp.concatenate([piece[: width // 2], piece[width // 2:]], axis=1)
    piece = lax.ppermute(piece, ("row", "col"), TO_COLUMN)
    cap_part = jnp.dot(columns_t, row_select.astype(F32), precision=HIGH, preferred_element_type=F32)
    cap_part = jnp.concatenate([cap_part[: BR // 2], cap_part[BR // 2:]], axis=1)
    mine = jnp.concatenate([piece, cap_part], axis=0)
    other = lax.ppermute(mine, "row", OTHER_Y)
    h = width // 2
    both = jnp.concatenate(
        [in_order(y, mine[:h], other[:h]).reshape(Y * h, 2 * BR), mine[h:] + other[h:]], axis=0
    )
    line = lax.all_gather(both, "row", axis_index_groups=ALONG_Z, axis=0)
    other_line = lax.ppermute(line, "row", OTHER_CORE)
    capacity = jnp.sum(line[:, Y * h:] + other_line[:, Y * h:], axis=0)
    capacity = jnp.concatenate([capacity[:, :BR], capacity[:, BR:]], axis=0)
    ends = in_order(core, line[:, : Y * h], other_line[:, : Y * h])
    ends = ends.reshape(CORES, Z, Y, h, 2, BR).transpose(2, 1, 0, 4, 3, 5).reshape(col_count, BR)

    other_columns_t = lax.ppermute(columns_t, "row", OTHER_CORE)
    both_columns_t = jnp.concatenate([columns_t, other_columns_t], axis=1)
    reach = impedance * (1.0 + 3.0 * switch_flags.astype(F32))
    factor = jnp.linalg.cholesky(capacity + jnp.diag(reach))
    solved = jax.scipy.linalg.cho_solve((factor, True), both_columns_t)

    correction = lax.dot_general(
        solved, ends, (((0,), (1,)), ((), ())), precision=HIGH, preferred_element_type=F32
    )
    after = jnp.concatenate([sensitivity, other_rows], axis=0) - correction
    after_high, after_low = split(after)

    zs = Z * Y // COLS
    sums = []
    for side in range(Y):
        part_loads = gathered[:, side].reshape(Z * slots, col_count)
        sums.append(nt(part_loads, after_high) + nt(part_loads, after_low))
    sums = jnp.stack(sums).reshape(COLS, zs * slots, CORES * row_count)
    arrived = lax.all_to_all(sums, "col", 0, 0, tiled=True)
    total = jnp.sum(arrived, axis=0)
    keep, give = total[:, :row_count], total[:, row_count:]
    taken = lax.ppermute(give, "row", OTHER_CORE)
    result = in_order(core, keep, taken).reshape(CORES, zs, slots, row_count)
    return result.transpose(3, 1, 0, 2).reshape(row_count, zs * CORES * slots)


def solution(mesh):
    placed = (P("row", "col"), P("col", "row"), P(), P(), P(), P())
    return jax.shard_map(
        on_device, mesh=mesh, in_specs=placed, out_specs=P("row", "col"), check_vma=False
    )
```

```python
import jax
import jax.numpy as jnp
from jax import lax
from jax.sharding import PartitionSpec as P

HIGH = lax.Precision.HIGHEST
F32 = jnp.float32
BF16 = jnp.bfloat16

Y, Z, CORES = 2, 16, 2
COLS = 8
BR = 64


def row_of(y, z, core):
    return y * Z * CORES + z * CORES + core


ROWS = [(y, z, core) for y in range(Y) for z in range(Z) for core in range(CORES)]
OTHER_CORE = [(row_of(y, z, k), row_of(y, z, 1 - k)) for y, z, k in ROWS]
OTHER_Y = [(row_of(y, z, k), row_of(1 - y, z, k)) for y, z, k in ROWS]
ALONG_Z = [[row_of(y, z, k) for z in range(Z)] for y in range(Y) for k in range(CORES)]
TO_COLUMN = [
    ((8 * a + b) * COLS + c, (8 * b + c) * COLS + a)
    for a in range(8) for b in range(8) for c in range(8)
]


def incidence_of(node_ids, from_node, to_node):
    plus = (node_ids[:, None] == from_node[None, :]).astype(BF16)
    minus = (node_ids[:, None] == to_node[None, :]).astype(BF16)
    return plus - minus


def split(values):
    high = lax.reduce_precision(values, 8, 7)
    return high.astype(BF16), (values - high).astype(BF16)


def in_order(position, mine, other):
    return jnp.where(position == 0, jnp.stack([mine, other]), jnp.stack([other, mine]))


def nt(left, right):
    return lax.dot_general(left, right, (((1,), (1,)), ((), ())), preferred_element_type=F32)


def on_device(sensitivity, injections, from_node, to_node, switch_flags, impedance):
    row_count, col_count = sensitivity.shape
    row = lax.axis_index("row")
    col = lax.axis_index("col")
    y, core = row // (Z * CORES), row % CORES
    slots = injections.shape[1]

    loads = injections.T
    other_loads = lax.ppermute(loads, "row", OTHER_Y)
    pair = in_order(y, loads, other_loads)
    gathered = lax.all_gather(pair, "row", axis_index_groups=ALONG_Z, axis=0)

    other_rows = lax.ppermute(sensitivity, "row", OTHER_CORE)

    high, low = split(sensitivity)
    col_select = incidence_of(col * col_count + jnp.arange(col_count, dtype=jnp.int32), from_node, to_node)
    row_select = incidence_of(row * row_count + jnp.arange(row_count, dtype=jnp.int32), from_node, to_node)
    part = nt(col_select.T, high) + nt(col_select.T, low)
    parts = lax.all_to_all(jnp.broadcast_to(part[None], (COLS,) + part.shape), "col", 0, 0, tiled=True)
    columns_t = jnp.sum(parts, axis=0)

    width = row_count // COLS
    piece = lax.dynamic_slice_in_dim(columns_t.T, col * width, width, 0)
    piece = jnp.concatenate([piece[: width // 2], piece[width // 2:]], axis=1)
    piece = lax.ppermute(piece, ("row", "col"), TO_COLUMN)
    cap_part = jnp.dot(columns_t, row_select.astype(F32), precision=HIGH, preferred_element_type=F32)
    cap_part = jnp.concatenate([cap_part[: BR // 2], cap_part[BR // 2:]], axis=1)
    mine = jnp.concatenate([piece, cap_part], axis=0)
    other = lax.ppermute(mine, "row", OTHER_Y)
    h = width // 2
    both = jnp.concatenate(
        [in_order(y, mine[:h], other[:h]).reshape(Y * h, 2 * BR), mine[h:] + other[h:]], axis=0
    )
    line = lax.all_gather(both, "row", axis_index_groups=ALONG_Z, axis=0)
    other_line = lax.ppermute(line, "row", OTHER_CORE)
    capacity = jnp.sum(line[:, Y * h:] + other_line[:, Y * h:], axis=0)
    capacity = jnp.concatenate([capacity[:, :BR], capacity[:, BR:]], axis=0)
    ends = in_order(core, line[:, : Y * h], other_line[:, : Y * h])
    ends = ends.reshape(CORES, Z, Y, h, 2, BR).transpose(2, 1, 0, 4, 3, 5).reshape(col_count, BR)

    other_high, other_low = split(other_rows)
    both_high = jnp.concatenate([high, other_high], axis=0)
    both_low = jnp.concatenate([low, other_low], axis=0)
    ends = jnp.concatenate(split(ends), axis=1)
    zs = Z * Y // COLS
    count = zs * slots
    sums, end_sums = [], []
    for side in range(Y):
        part_loads = gathered[:, side].reshape(Z * slots, col_count)
        sums.append(nt(part_loads, both_high) + nt(part_loads, both_low))
        end_part = jnp.dot(part_loads, ends, preferred_element_type=F32)
        end_sums.append(end_part[:, :BR] + end_part[:, BR:])
    sums = jnp.stack(sums).reshape(COLS, count, CORES * row_count)
    fold = CORES * row_count // BR
    end_sums = jnp.stack(end_sums).reshape(COLS, fold, count // fold, BR)
    end_sums = end_sums.transpose(0, 2, 1, 3).reshape(COLS, count // fold, fold * BR)
    arrived = lax.all_to_all(jnp.concatenate([sums, end_sums], axis=1), "col", 0, 0, tiled=True)

    reach = impedance * (1.0 + 3.0 * switch_flags.astype(F32))
    factor = jnp.linalg.cholesky(capacity + jnp.diag(reach))
    solved = jax.scipy.linalg.cho_solve((factor, True), columns_t)

    total = jnp.sum(arrived, axis=0)
    end_total = total[count:].reshape(count // fold, fold, BR).transpose(1, 0, 2).reshape(count, BR)
    mine = jnp.concatenate([total[:count, :row_count], end_total], axis=1)
    give = jnp.concatenate([total[:count, row_count:], end_total], axis=1)
    taken = lax.ppermute(give, "row", OTHER_CORE)
    result = in_order(core, mine, taken).reshape(CORES, zs, slots, row_count + BR)
    result = result.transpose(1, 0, 2, 3).reshape(CORES * count, row_count + BR)
    drop = lax.dot_general(
        solved, result[:, row_count:], (((0,), (1,)), ((), ())), precision=HIGH, preferred_element_type=F32
    )
    return result[:, :row_count].T - drop


def solution(mesh):
    placed = (P("row", "col"), P("col", "row"), P(), P(), P(), P())
    return jax.shard_map(
        on_device, mesh=mesh, in_specs=placed, out_specs=P("row", "col"), check_vma=False
    )
```

```python
import jax
import jax.numpy as jnp
from jax import lax
from jax.sharding import PartitionSpec as P

HIGH = lax.Precision.HIGHEST
F32 = jnp.float32
BF16 = jnp.bfloat16

Y, Z, CORES = 2, 16, 2
COLS = 8
BR = 64


def row_of(y, z, core):
    return y * Z * CORES + z * CORES + core


ROWS = [(y, z, core) for y in range(Y) for z in range(Z) for core in range(CORES)]
OTHER_CORE = [(row_of(y, z, k), row_of(y, z, 1 - k)) for y, z, k in ROWS]
OTHER_Y = [(row_of(y, z, k), row_of(1 - y, z, k)) for y, z, k in ROWS]
ALONG_Z_CORE = [[row_of(y, z, k) for z in range(Z) for k in range(CORES)] for y in range(Y)]
ALONG_Z = [[row_of(y, z, k) for z in range(Z)] for y in range(Y) for k in range(CORES)]
TO_COLUMN = [
    ((8 * a + b) * COLS + c, (8 * b + c) * COLS + a)
    for a in range(8) for b in range(8) for c in range(8)
]


def incidence_of(node_ids, from_node, to_node):
    plus = (node_ids[:, None] == from_node[None, :]).astype(BF16)
    minus = (node_ids[:, None] == to_node[None, :]).astype(BF16)
    return plus - minus


def split(values):
    high = lax.reduce_precision(values, 8, 7)
    return high.astype(BF16), (values - high).astype(BF16)


def in_order(position, mine, other):
    return jnp.where(position == 0, jnp.stack([mine, other]), jnp.stack([other, mine]))


def nt(left, right):
    return lax.dot_general(left, right, (((1,), (1,)), ((), ())), preferred_element_type=F32)


def on_device(sensitivity, injections, from_node, to_node, switch_flags, impedance):
    row_count, col_count = sensitivity.shape
    row = lax.axis_index("row")
    col = lax.axis_index("col")
    y, core = row // (Z * CORES), row % CORES
    slots = injections.shape[1]

    loads = injections.T
    other_loads = lax.ppermute(loads, "row", OTHER_Y)

    high, low = split(sensitivity)
    col_select = incidence_of(col * col_count + jnp.arange(col_count, dtype=jnp.int32), from_node, to_node)
    row_select = incidence_of(row * row_count + jnp.arange(row_count, dtype=jnp.int32), from_node, to_node)
    part = nt(col_select.T, high) + nt(col_select.T, low)
    part, other_loads = lax.optimization_barrier((part, other_loads))

    pair = in_order(y, loads, other_loads)
    gathered = lax.all_gather(pair, "row", axis_index_groups=ALONG_Z_CORE, axis=0)

    parts = lax.all_to_all(jnp.broadcast_to(part[None], (COLS,) + part.shape), "col", 0, 0, tiled=True)
    columns_t = jnp.sum(parts, axis=0)

    width = row_count // COLS
    piece = lax.dynamic_slice_in_dim(columns_t.T, col * width, width, 0)
    piece = jnp.concatenate([piece[: width // 2], piece[width // 2:]], axis=1)
    piece = lax.ppermute(piece, ("row", "col"), TO_COLUMN)
    cap_part = jnp.dot(columns_t, row_select.astype(F32), precision=HIGH, preferred_element_type=F32)
    cap_part = jnp.concatenate([cap_part[: BR // 2], cap_part[BR // 2:]], axis=1)
    mine = jnp.concatenate([piece, cap_part], axis=0)
    other = lax.ppermute(mine, "row", OTHER_Y)
    h = width // 2
    both = jnp.concatenate(
        [in_order(y, mine[:h], other[:h]).reshape(Y * h, 2 * BR), mine[h:] + other[h:]], axis=0
    )
    line = lax.all_gather(both, "row", axis_index_groups=ALONG_Z, axis=0)
    other_line = lax.ppermute(line, "row", OTHER_CORE)
    capacity = jnp.sum(line[:, Y * h:] + other_line[:, Y * h:], axis=0)
    capacity = jnp.concatenate([capacity[:, :BR], capacity[:, BR:]], axis=0)
    ends = in_order(core, line[:, : Y * h], other_line[:, : Y * h])
    ends = ends.reshape(CORES, Z, Y, h, 2, BR).transpose(2, 1, 0, 4, 3, 5).reshape(col_count, BR)

    ends = jnp.concatenate(split(ends), axis=1)
    everything = gathered.reshape(Z * CORES * Y * slots, col_count)
    sums = nt(everything, high) + nt(everything, low)
    end_sums = jnp.dot(everything, ends, preferred_element_type=F32)
    end_sums = end_sums[:, :BR] + end_sums[:, BR:]
    zs = Z * Y // COLS
    count = zs * CORES * slots

    def by_block(values):
        values = values.reshape(Z // zs, zs * CORES, Y, slots, values.shape[1]).transpose(2, 0, 1, 3, 4)
        return values.reshape(COLS, count, values.shape[4])

    fold = row_count // BR
    end_sums = by_block(end_sums).reshape(COLS, fold, count // fold, BR)
    end_sums = end_sums.transpose(0, 2, 1, 3).reshape(COLS, count // fold, fold * BR)
    packed = jnp.concatenate([by_block(sums), end_sums], axis=1)
    arrived = lax.all_to_all(packed, "col", 0, 0, tiled=True)

    reach = impedance * (1.0 + 3.0 * switch_flags.astype(F32))
    factor = jnp.linalg.cholesky(capacity + jnp.diag(reach))
    solved = jax.scipy.linalg.cho_solve((factor, True), columns_t)

    total = jnp.sum(arrived, axis=0)
    end_total = total[count:].reshape(count // fold, fold, BR).transpose(1, 0, 2).reshape(count, BR)
    drop = lax.dot_general(
        solved, end_total, (((0,), (1,)), ((), ())), precision=HIGH, preferred_element_type=F32
    )
    return total[:count].T - drop


def solution(mesh):
    placed = (P("row", "col"), P("col", "row"), P(), P(), P(), P())
    return jax.shard_map(
        on_device, mesh=mesh, in_specs=placed, out_specs=P("row", "col"), check_vma=False
    )
```

```python
import jax
import jax.numpy as jnp
from jax import lax
from jax.experimental import pallas as pl
from jax.experimental.pallas import tpu as pltpu
from jax.sharding import PartitionSpec as P

HIGH = lax.Precision.HIGHEST
F32 = jnp.float32
BF16 = jnp.bfloat16

Y, Z, CORES = 2, 16, 2
COLS = 8
BR = 64


def row_of(y, z, core):
    return y * Z * CORES + z * CORES + core


ROWS = [(y, z, core) for y in range(Y) for z in range(Z) for core in range(CORES)]
OTHER_CORE = [(row_of(y, z, k), row_of(y, z, 1 - k)) for y, z, k in ROWS]
OTHER_Y = [(row_of(y, z, k), row_of(1 - y, z, k)) for y, z, k in ROWS]
ALONG_Z_CORE = [[row_of(y, z, k) for z in range(Z) for k in range(CORES)] for y in range(Y)]
ALONG_Z = [[row_of(y, z, k) for z in range(Z)] for y in range(Y) for k in range(CORES)]
TO_COLUMN = [
    ((8 * a + b) * COLS + c, (8 * b + c) * COLS + a)
    for a in range(8) for b in range(8) for c in range(8)
]


def incidence_of(node_ids, from_node, to_node):
    plus = (node_ids[:, None] == from_node[None, :]).astype(BF16)
    minus = (node_ids[:, None] == to_node[None, :]).astype(BF16)
    return plus - minus


def split(values):
    high = lax.reduce_precision(values, 8, 7)
    return high.astype(BF16), (values - high).astype(BF16)


def in_order(position, mine, other):
    return jnp.where(position == 0, jnp.stack([mine, other]), jnp.stack([other, mine]))


def nt(left, right):
    return lax.dot_general(left, right, (((1,), (1,)), ((), ())), preferred_element_type=F32)


def products(loads, weights, ends):
    blocks, lines, sides, slots, nodes = loads.shape
    rows = weights.shape[1] // 2
    count = lines * slots
    fold = rows // BR

    def body(loads_ref, weights_ref, ends_ref, out_ref):
        tile = loads_ref[...].reshape(count, nodes)
        sums = jnp.dot(tile, weights_ref[...], preferred_element_type=F32)
        out_ref[0, :count] = sums[:, :rows] + sums[:, rows:]
        end_sums = jnp.dot(tile, ends_ref[...], preferred_element_type=F32)
        end_sums = end_sums[:, :BR] + end_sums[:, BR:]
        step = count // fold
        folded = [end_sums[i * step:(i + 1) * step] for i in range(fold)]
        out_ref[0, count:] = jnp.concatenate(folded, axis=1)

    height = count + count // fold
    return pl.pallas_call(
        body,
        grid=(sides, blocks),
        in_specs=[
            pl.BlockSpec((1, lines, 1, slots, nodes), lambda side, block: (block, 0, side, 0, 0)),
            pl.BlockSpec(weights.shape, lambda side, block: (0, 0)),
            pl.BlockSpec(ends.shape, lambda side, block: (0, 0)),
        ],
        out_specs=pl.BlockSpec((1, height, rows), lambda side, block: (side * blocks + block, 0, 0)),
        out_shape=jax.ShapeDtypeStruct((sides * blocks, height, rows), F32),
        compiler_params=pltpu.CompilerParams(vmem_limit_bytes=32 * 1024 * 1024),
    )(loads, weights, ends)


def on_device(sensitivity, injections, from_node, to_node, switch_flags, impedance):
    row_count, col_count = sensitivity.shape
    row = lax.axis_index("row")
    col = lax.axis_index("col")
    y, core = row // (Z * CORES), row % CORES
    slots = injections.shape[1]

    loads = injections.T
    other_loads = lax.ppermute(loads, "row", OTHER_Y)

    high, low = split(sensitivity)
    col_select = incidence_of(col * col_count + jnp.arange(col_count, dtype=jnp.int32), from_node, to_node)
    row_select = incidence_of(row * row_count + jnp.arange(row_count, dtype=jnp.int32), from_node, to_node)
    part = nt(col_select.T, high) + nt(col_select.T, low)
    part, other_loads = lax.optimization_barrier((part, other_loads))
    weights = jnp.concatenate([high.T, low.T], axis=1)

    pair = in_order(y, loads, other_loads)
    gathered = lax.all_gather(pair, "row", axis_index_groups=ALONG_Z_CORE, axis=0)

    parts = lax.all_to_all(jnp.broadcast_to(part[None], (COLS,) + part.shape), "col", 0, 0, tiled=True)
    columns_t = jnp.sum(parts, axis=0)

    width = row_count // COLS
    piece = lax.dynamic_slice_in_dim(columns_t.T, col * width, width, 0)
    piece = jnp.concatenate([piece[: width // 2], piece[width // 2:]], axis=1)
    piece = lax.ppermute(piece, ("row", "col"), TO_COLUMN)
    cap_part = jnp.dot(columns_t, row_select.astype(F32), precision=HIGH, preferred_element_type=F32)
    cap_part = jnp.concatenate([cap_part[: BR // 2], cap_part[BR // 2:]], axis=1)
    mine = jnp.concatenate([piece, cap_part], axis=0)
    other = lax.ppermute(mine, "row", OTHER_Y)
    h = width // 2
    both = jnp.concatenate(
        [in_order(y, mine[:h], other[:h]).reshape(Y * h, 2 * BR), mine[h:] + other[h:]], axis=0
    )
    line = lax.all_gather(both, "row", axis_index_groups=ALONG_Z, axis=0)
    other_line = lax.ppermute(line, "row", OTHER_CORE)
    capacity = jnp.sum(line[:, Y * h:] + other_line[:, Y * h:], axis=0)
    capacity = jnp.concatenate([capacity[:, :BR], capacity[:, BR:]], axis=0)
    ends = in_order(core, line[:, : Y * h], other_line[:, : Y * h])
    ends = ends.reshape(CORES, Z, Y, h, 2, BR).transpose(2, 1, 0, 4, 3, 5).reshape(col_count, BR)

    zs = Z * Y // COLS
    count = zs * CORES * slots
    fold = row_count // BR
    packed = products(
        gathered.reshape(Z // zs, zs * CORES, Y, slots, col_count),
        weights,
        jnp.concatenate(split(ends), axis=1),
    )
    arrived = lax.all_to_all(packed, "col", 0, 0, tiled=True)

    reach = impedance * (1.0 + 3.0 * switch_flags.astype(F32))
    factor = jnp.linalg.cholesky(capacity + jnp.diag(reach))
    solved = jax.scipy.linalg.cho_solve((factor, True), columns_t)

    total = jnp.sum(arrived, axis=0)
    end_total = total[count:].reshape(count // fold, fold, BR).transpose(1, 0, 2).reshape(count, BR)
    drop = lax.dot_general(
        solved, end_total, (((0,), (1,)), ((), ())), precision=HIGH, preferred_element_type=F32
    )
    return total[:count].T - drop


def solution(mesh):
    placed = (P("row", "col"), P("col", "row"), P(), P(), P(), P())
    return jax.shard_map(
        on_device, mesh=mesh, in_specs=placed, out_specs=P("row", "col"), check_vma=False
    )
```

```python
import jax
import jax.numpy as jnp
from jax import lax
from jax.experimental import pallas as pl
from jax.experimental.pallas import tpu as pltpu
from jax.sharding import PartitionSpec as P

HIGH = lax.Precision.HIGHEST
F32 = jnp.float32
BF16 = jnp.bfloat16

Y, Z, CORES = 2, 16, 2
COLS = 8
BR = 64


def row_of(y, z, core):
    return y * Z * CORES + z * CORES + core


ROWS = [(y, z, core) for y in range(Y) for z in range(Z) for core in range(CORES)]
OTHER_CORE = [(row_of(y, z, k), row_of(y, z, 1 - k)) for y, z, k in ROWS]
OTHER_Y = [(row_of(y, z, k), row_of(1 - y, z, k)) for y, z, k in ROWS]
ALONG_Z_CORE = [[row_of(y, z, k) for z in range(Z) for k in range(CORES)] for y in range(Y)]
ALONG_Z = [[row_of(y, z, k) for z in range(Z)] for y in range(Y) for k in range(CORES)]
TO_COLUMN = [
    ((8 * a + b) * COLS + c, (8 * b + c) * COLS + a)
    for a in range(8) for b in range(8) for c in range(8)
]


def incidence_of(node_ids, from_node, to_node):
    plus = (node_ids[:, None] == from_node[None, :]).astype(BF16)
    minus = (node_ids[:, None] == to_node[None, :]).astype(BF16)
    return plus - minus


def split(values):
    high = lax.reduce_precision(values, 8, 7)
    return high.astype(BF16), (values - high).astype(BF16)


def in_order(position, mine, other):
    return jnp.where(position == 0, jnp.stack([mine, other]), jnp.stack([other, mine]))


def nt(left, right):
    return lax.dot_general(left, right, (((1,), (1,)), ((), ())), preferred_element_type=F32)


def products(loads, weights, ends):
    blocks, lines, sides, slots, nodes = loads.shape
    rows = weights.shape[1] // 2
    count = lines * slots
    fold = rows // BR

    taken = 2

    def body(loads_ref, weights_ref, ends_ref, out_ref):
        tile = loads_ref[...].reshape(taken * count, nodes)
        sums = jnp.dot(tile, weights_ref[...], preferred_element_type=F32)
        sums = sums[:, :rows] + sums[:, rows:]
        end_sums = jnp.dot(tile, ends_ref[...], preferred_element_type=F32)
        end_sums = end_sums[:, :BR] + end_sums[:, BR:]
        step = count // fold
        for block in range(taken):
            at = block * count
            out_ref[block, :count] = sums[at:at + count]
            folded = [end_sums[at + i * step:at + (i + 1) * step] for i in range(fold)]
            out_ref[block, count:] = jnp.concatenate(folded, axis=1)

    height = count + count // fold
    return pl.pallas_call(
        body,
        grid=(sides, blocks // taken),
        in_specs=[
            pl.BlockSpec((taken, lines, 1, slots, nodes), lambda side, block: (block, 0, side, 0, 0)),
            pl.BlockSpec(weights.shape, lambda side, block: (0, 0)),
            pl.BlockSpec(ends.shape, lambda side, block: (0, 0)),
        ],
        out_specs=pl.BlockSpec((taken, height, rows), lambda side, block: (side * (blocks // taken) + block, 0, 0)),
        out_shape=jax.ShapeDtypeStruct((sides * blocks, height, rows), F32),
        compiler_params=pltpu.CompilerParams(vmem_limit_bytes=56 * 1024 * 1024),
    )(loads, weights, ends)


def on_device(sensitivity, injections, from_node, to_node, switch_flags, impedance):
    row_count, col_count = sensitivity.shape
    row = lax.axis_index("row")
    col = lax.axis_index("col")
    y, core = row // (Z * CORES), row % CORES
    slots = injections.shape[1]

    loads = injections.T
    other_loads = lax.ppermute(loads, "row", OTHER_Y)

    high, low = split(sensitivity)
    col_select = incidence_of(col * col_count + jnp.arange(col_count, dtype=jnp.int32), from_node, to_node)
    row_select = incidence_of(row * row_count + jnp.arange(row_count, dtype=jnp.int32), from_node, to_node)
    part = nt(col_select.T, high) + nt(col_select.T, low)
    reach_of_rows = jnp.sum(jnp.abs(sensitivity), axis=1)
    part = jnp.concatenate([part, jnp.broadcast_to(reach_of_rows[None], (8, row_count))], axis=0)
    part, other_loads = lax.optimization_barrier((part, other_loads))
    weights = jnp.concatenate([high.T, low.T], axis=1)

    pair = in_order(y, loads, other_loads)
    gathered = lax.all_gather(pair, "row", axis_index_groups=ALONG_Z_CORE, axis=0)

    parts = lax.all_to_all(jnp.broadcast_to(part[None], (COLS,) + part.shape), "col", 0, 0, tiled=True)
    parts = jnp.sum(parts, axis=0)
    parts, weights = lax.optimization_barrier((parts, weights))
    columns_t, row_bound = parts[:BR], parts[BR:]

    width = row_count // COLS
    piece = lax.dynamic_slice_in_dim(columns_t.T, col * width, width, 0)
    piece = jnp.concatenate([piece[: width // 2], piece[width // 2:]], axis=1)
    piece = lax.ppermute(piece, ("row", "col"), TO_COLUMN)
    cap_part = jnp.dot(columns_t, row_select.astype(F32), precision=HIGH, preferred_element_type=F32)
    cap_part = jnp.concatenate([cap_part[: BR // 2], cap_part[BR // 2:]], axis=1)
    end_bound = jnp.dot(row_bound, jnp.abs(row_select.astype(F32)), precision=HIGH, preferred_element_type=F32)
    mine = jnp.concatenate([piece, cap_part, jnp.concatenate([end_bound, end_bound], axis=1)], axis=0)
    other = lax.ppermute(mine, "row", OTHER_Y)
    h = width // 2
    both = jnp.concatenate(
        [in_order(y, mine[:h], other[:h]).reshape(Y * h, 2 * BR), mine[h:] + other[h:]], axis=0
    )
    line = lax.all_gather(both, "row", axis_index_groups=ALONG_Z, axis=0)
    other_line = lax.ppermute(line, "row", OTHER_CORE)
    capacity = jnp.sum(line[:, Y * h:] + other_line[:, Y * h:], axis=0)
    end_bound = capacity[BR // 2, :BR]
    capacity = jnp.concatenate([capacity[: BR // 2, :BR], capacity[: BR // 2, BR:]], axis=0)
    ends = in_order(core, line[:, : Y * h], other_line[:, : Y * h])
    ends = ends.reshape(CORES, Z, Y, h, 2, BR).transpose(2, 1, 0, 4, 3, 5).reshape(col_count, BR)

    zs = Z * Y // COLS
    count = zs * CORES * slots
    fold = row_count // BR
    packed = products(
        gathered.reshape(Z // zs, zs * CORES, Y, slots, col_count),
        weights,
        jnp.concatenate(split(ends), axis=1),
    )
    bound = jnp.concatenate([
        jnp.broadcast_to(row_bound[:1], (count, row_count)),
        jnp.broadcast_to(jnp.concatenate([end_bound] * fold)[None], (count // fold, row_count)),
    ])
    bound = jnp.maximum(bound, 1e-30) / 8192.0
    arrived = lax.all_to_all((packed / bound).astype(jnp.float16), "col", 0, 0, tiled=True)

    reach = impedance * (1.0 + 3.0 * switch_flags.astype(F32))
    factor = jnp.linalg.cholesky(capacity + jnp.diag(reach))
    solved = jax.scipy.linalg.cho_solve((factor, True), columns_t)

    total = jnp.sum(arrived.astype(F32), axis=0) * bound
    end_total = total[count:].reshape(count // fold, fold, BR).transpose(1, 0, 2).reshape(count, BR)
    drop = lax.dot_general(
        solved, end_total, (((0,), (1,)), ((), ())), precision=HIGH, preferred_element_type=F32
    )
    return total[:count].T - drop


def solution(mesh):
    placed = (P("row", "col"), P("col", "row"), P(), P(), P(), P())
    return jax.shard_map(
        on_device, mesh=mesh, in_specs=placed, out_specs=P("row", "col"), check_vma=False
    )
```

```python
import jax
import jax.numpy as jnp
from jax import lax
from jax.experimental import pallas as pl
from jax.experimental.pallas import tpu as pltpu
from jax.sharding import PartitionSpec as P

HIGH = lax.Precision.HIGHEST
F32 = jnp.float32
BF16 = jnp.bfloat16

Y, Z, CORES = 2, 16, 2
COLS = 8
BR = 64


def row_of(y, z, core):
    return y * Z * CORES + z * CORES + core


ROWS = [(y, z, core) for y in range(Y) for z in range(Z) for core in range(CORES)]
OTHER_Y = [(row_of(y, z, k), row_of(1 - y, z, k)) for y, z, k in ROWS]
ALONG_Z_CORE = [[row_of(y, z, k) for z in range(Z) for k in range(CORES)] for y in range(Y)]
Q = 4
ACROSS_QUARTERS = [
    [row_of(y, q * Q + i, k) for q in range(Z // Q)] for y in range(Y) for i in range(Q) for k in range(CORES)
]
QUARTERS = [
    [row_of(y, q * Q + i, k) for i in range(Q)] for y in range(Y) for q in range(Z // Q) for k in range(CORES)
]
CHIP_PAIRS = [[row_of(y, z, k) for y in range(Y) for k in range(CORES)] for z in range(Z)]
TO_COLUMN = [
    ((8 * a + b) * COLS + c, (8 * b + c) * COLS + a)
    for a in range(8) for b in range(8) for c in range(8)
]


def incidence_of(node_ids, from_node, to_node):
    plus = (node_ids[:, None] == from_node[None, :]).astype(BF16)
    minus = (node_ids[:, None] == to_node[None, :]).astype(BF16)
    return plus - minus


def split(values):
    high = lax.reduce_precision(values, 8, 7)
    return high.astype(BF16), (values - high).astype(BF16)


def in_order(position, mine, other):
    return jnp.where(position == 0, jnp.stack([mine, other]), jnp.stack([other, mine]))


def nt(left, right):
    return lax.dot_general(left, right, (((1,), (1,)), ((), ())), preferred_element_type=F32)


def gather(values, groups):
    copies = jnp.broadcast_to(values[None], (len(groups[0]),) + values.shape)
    return lax.all_to_all(copies, "row", 0, 0, axis_index_groups=groups, tiled=True)


def products(loads, weights):
    blocks, lines, sides, slots, nodes = loads.shape
    rows = weights.shape[0] // 2
    count = lines * slots
    taken = 2

    def body(loads_ref, weights_ref, out_ref):
        tile = loads_ref[...].reshape(taken * count, nodes)
        sums = nt(tile, weights_ref[...])
        sums = sums[:, :rows] + sums[:, rows:]
        out_ref[...] = sums.reshape(taken, count, rows)

    return pl.pallas_call(
        body,
        grid=(sides, blocks // taken),
        in_specs=[
            pl.BlockSpec((taken, lines, 1, slots, nodes), lambda side, block: (block, 0, side, 0, 0)),
            pl.BlockSpec(weights.shape, lambda side, block: (0, 0)),
        ],
        out_specs=pl.BlockSpec((taken, count, rows), lambda side, block: (side * (blocks // taken) + block, 0, 0)),
        out_shape=jax.ShapeDtypeStruct((sides * blocks, count, rows), F32),
        compiler_params=pltpu.CompilerParams(vmem_limit_bytes=56 * 1024 * 1024),
    )(loads, weights)


def on_device(sensitivity, injections, from_node, to_node, switch_flags, impedance):
    row_count, col_count = sensitivity.shape
    row = lax.axis_index("row")
    col = lax.axis_index("col")
    y, core = row // (Z * CORES), row % CORES
    slots = injections.shape[1]

    loads = injections.T
    other_loads = lax.ppermute(loads, "row", OTHER_Y)

    high, low = split(sensitivity)
    col_select = incidence_of(col * col_count + jnp.arange(col_count, dtype=jnp.int32), from_node, to_node)
    row_select = incidence_of(row * row_count + jnp.arange(row_count, dtype=jnp.int32), from_node, to_node)
    part = nt(col_select.T, high) + nt(col_select.T, low)
    reach_of_rows = jnp.sum(jnp.abs(sensitivity), axis=1)
    part = jnp.concatenate([part, jnp.broadcast_to(reach_of_rows[None], (8, row_count))], axis=0)
    part, other_loads = lax.optimization_barrier((part, other_loads))

    pair = in_order(y, loads, other_loads)
    gathered = lax.all_gather(pair, "row", axis_index_groups=ALONG_Z_CORE, axis=0)

    parts = lax.all_to_all(jnp.broadcast_to(part[None], (COLS,) + part.shape), "col", 0, 0, tiled=True)
    parts = jnp.sum(parts, axis=0)
    columns_t, row_bound = parts[:BR], parts[BR:]

    width = row_count // COLS
    piece = lax.dynamic_slice_in_dim(columns_t.T, col * width, width, 0)
    piece = jnp.concatenate([piece[: width // 2], piece[width // 2:]], axis=1)
    piece = lax.ppermute(piece, ("row", "col"), TO_COLUMN)
    cap_part = jnp.dot(columns_t, row_select.astype(F32), precision=HIGH, preferred_element_type=F32)
    cap_part = jnp.concatenate([cap_part[: BR // 2], cap_part[BR // 2:]], axis=1)
    end_bound = jnp.dot(row_bound, jnp.abs(row_select.astype(F32)), precision=HIGH, preferred_element_type=F32)
    h = width // 2
    mine = jnp.concatenate([piece, cap_part, jnp.concatenate([end_bound, end_bound], axis=1)], axis=0)
    for groups in (ACROSS_QUARTERS, QUARTERS, CHIP_PAIRS):
        got = gather(mine, groups)
        top = mine.shape[0] - BR // 2 - 8
        mine = jnp.concatenate([got[:, :top].reshape(-1, 2 * BR), jnp.sum(got[:, top:], axis=0)], axis=0)
    top = mine.shape[0] - BR // 2 - 8
    ends = mine[:top].reshape(Y, CORES, Q, Z // Q, h, 2, BR)
    ends = ends.transpose(0, 3, 2, 1, 5, 4, 6).reshape(col_count, BR)
    capacity = jnp.concatenate([mine[top:-8, :BR], mine[top:-8, BR:]], axis=0)
    end_bound = mine[-8:, :BR]

    reach = impedance * (1.0 + 3.0 * switch_flags.astype(F32))
    factor = jnp.linalg.cholesky(capacity + jnp.diag(reach))
    solved = jax.scipy.linalg.cho_solve((factor, True), columns_t)
    bound = row_bound + jnp.dot(end_bound, jnp.abs(solved), precision=HIGH, preferred_element_type=F32)
    unit = jnp.maximum(bound[0], 1e-30) / 8192.0
    correction = lax.dot_general(
        solved, ends, (((0,), (1,)), ((), ())), precision=HIGH, preferred_element_type=F32
    )
    weights = jnp.concatenate(split((sensitivity - correction) * (1.0 / unit)[:, None]), axis=0)

    zs = Z * Y // COLS
    count = zs * CORES * slots
    packed = products(gathered.reshape(Z // zs, zs * CORES, Y, slots, col_count), weights)
    arrived = lax.all_to_all(packed.astype(jnp.float16), "col", 0, 0, tiled=True)
    total = jnp.sum(arrived.astype(F32), axis=0) * unit[None]
    return total.T


def solution(mesh):
    placed = (P("row", "col"), P("col", "row"), P(), P(), P(), P())
    return jax.shard_map(
        on_device, mesh=mesh, in_specs=placed, out_specs=P("row", "col"), check_vma=False
    )
```

```python
import jax
import jax.numpy as jnp
from jax import lax
from jax.experimental import pallas as pl
from jax.experimental.pallas import tpu as pltpu
from jax.sharding import PartitionSpec as P

HIGH = lax.Precision.HIGHEST
F32 = jnp.float32
BF16 = jnp.bfloat16

Y, Z, CORES = 2, 16, 2
COLS = 8
BR = 64


def row_of(y, z, core):
    return y * Z * CORES + z * CORES + core


ROWS = [(y, z, core) for y in range(Y) for z in range(Z) for core in range(CORES)]
OTHER_Y = [(row_of(y, z, k), row_of(1 - y, z, k)) for y, z, k in ROWS]
ALONG_Z_CORE = [[row_of(y, z, k) for z in range(Z) for k in range(CORES)] for y in range(Y)]
ALONG_Z = [[row_of(y, z, k) for z in range(Z)] for y in range(Y) for k in range(CORES)]
OTHER_CORE = [(row_of(y, z, k), row_of(y, z, 1 - k)) for y, z, k in ROWS]


def incidence_of(node_ids, from_node, to_node):
    plus = (node_ids[:, None] == from_node[None, :]).astype(BF16)
    minus = (node_ids[:, None] == to_node[None, :]).astype(BF16)
    return plus - minus


def split(values):
    high = lax.reduce_precision(values, 8, 7)
    return high.astype(BF16), (values - high).astype(BF16)


def in_order(position, mine, other):
    return jnp.where(position == 0, jnp.stack([mine, other]), jnp.stack([other, mine]))


def nt(left, right):
    return lax.dot_general(left, right, (((1,), (1,)), ((), ())), preferred_element_type=F32)


def products(loads, high, low):
    blocks, lines, sides, slots, nodes = loads.shape
    rows = high.shape[0]
    count = lines * slots
    taken = 2

    def body(loads_ref, high_ref, low_ref, out_ref):
        tile = loads_ref[...].reshape(taken * count, nodes)
        out_ref[...] = (nt(tile, high_ref[...]) + nt(tile, low_ref[...])).reshape(taken, count, rows)

    return pl.pallas_call(
        body,
        grid=(sides, blocks // taken),
        in_specs=[
            pl.BlockSpec((taken, lines, 1, slots, nodes), lambda side, block: (block, 0, side, 0, 0)),
            pl.BlockSpec(high.shape, lambda side, block: (0, 0)),
            pl.BlockSpec(low.shape, lambda side, block: (0, 0)),
        ],
        out_specs=pl.BlockSpec((taken, count, rows), lambda side, block: (side * (blocks // taken) + block, 0, 0)),
        out_shape=jax.ShapeDtypeStruct((sides * blocks, count, rows), F32),
        compiler_params=pltpu.CompilerParams(vmem_limit_bytes=56 * 1024 * 1024),
    )(loads, high, low)


def solve(matrix, right):
    size = matrix.shape[0]

    def body(matrix_ref, right_ref, out_ref):
        left, right = matrix_ref[...], right_ref[...]
        index = lax.broadcasted_iota(jnp.int32, (size, 1), 0)
        for k in range(size):
            inverse = 1.0 / left[k:k + 1, k:k + 1]
            left_row, right_row = left[k:k + 1] * inverse, right[k:k + 1] * inverse
            column = left[:, k:k + 1]
            here = index == k
            left = jnp.where(here, left_row, left - column * left_row)
            right = jnp.where(here, right_row, right - column * right_row)
        out_ref[...] = right

    return pl.pallas_call(body, out_shape=jax.ShapeDtypeStruct(right.shape, F32))(matrix, right)


def on_device(sensitivity, injections, from_node, to_node, switch_flags, impedance):
    row_count, col_count = sensitivity.shape
    row = lax.axis_index("row")
    col = lax.axis_index("col")
    y, core = row // (Z * CORES), row % CORES
    slots = injections.shape[1]

    loads = injections.T
    other_loads = lax.ppermute(loads, "row", OTHER_Y)

    high, low = split(sensitivity)
    col_select = incidence_of(col * col_count + jnp.arange(col_count, dtype=jnp.int32), from_node, to_node)
    row_select = incidence_of(row * row_count + jnp.arange(row_count, dtype=jnp.int32), from_node, to_node)
    part = nt(col_select.T, high) + nt(col_select.T, low)
    reach_of_rows = jnp.sum(jnp.abs(sensitivity), axis=1)
    part = jnp.concatenate([part, jnp.broadcast_to(reach_of_rows[None], (8, row_count))], axis=0)
    part, other_loads = lax.optimization_barrier((part, other_loads))

    pair = in_order(y, loads, other_loads)
    gathered = lax.all_gather(pair, "row", axis_index_groups=ALONG_Z_CORE, axis=0)

    parts = lax.all_to_all(jnp.broadcast_to(part[None], (COLS,) + part.shape), "col", 0, 0, tiled=True)
    parts = jnp.sum(parts, axis=0)
    columns_t, row_bound = parts[:BR], parts[BR:]

    half = row_count // 2
    first, second = columns_t[:, :half], columns_t[:, half:]
    cap_part = jnp.dot(columns_t, row_select.astype(F32), precision=HIGH, preferred_element_type=F32)
    cap_part = jnp.concatenate([cap_part[: BR // 2], cap_part[BR // 2:]], axis=1)
    end_bound = jnp.dot(row_bound, jnp.abs(row_select.astype(F32)), precision=HIGH, preferred_element_type=F32)
    cap_part = jnp.concatenate([cap_part, jnp.concatenate([end_bound, end_bound], axis=1)], axis=0)
    give = jnp.concatenate([jnp.where(y == 0, second, first), cap_part], axis=0)
    take = lax.ppermute(give, "row", OTHER_Y)
    blocks = COLS // Y
    block = jnp.where(col // blocks == y, jnp.where(y == 0, first, second), take[:BR])
    line = lax.all_gather(
        jnp.concatenate([block, cap_part + take[BR:]], axis=0), "row", axis_index_groups=ALONG_Z, axis=0
    )
    zs = Z // blocks
    ends = lax.dynamic_slice_in_dim(line[:, :BR], (col % blocks) * zs, zs, 0).reshape(zs * BR, half)
    mine = jnp.concatenate([ends, jnp.sum(line[:, BR:], axis=0)], axis=0)
    other = lax.ppermute(mine, "row", OTHER_CORE)
    ends = in_order(core, mine[: zs * BR], other[: zs * BR])
    other_ends = lax.ppermute(ends, "row", OTHER_Y)
    capacity = mine[zs * BR:] + other[zs * BR:]
    end_bound = capacity[BR // 2:, :BR]
    capacity = jnp.concatenate([capacity[: BR // 2, :BR], capacity[: BR // 2, BR:]], axis=0)

    reach = impedance * (1.0 + 3.0 * switch_flags.astype(F32))
    solved = solve(capacity + jnp.diag(reach), columns_t)
    bound = row_bound + jnp.dot(end_bound, jnp.abs(solved), precision=HIGH, preferred_element_type=F32)
    unit = jnp.maximum(bound[0], 1e-30) / 8192.0
    ends = in_order(y, ends, other_ends).reshape(Y, CORES, zs, BR, half)
    ends = ends.transpose(3, 2, 1, 0, 4).reshape(BR, col_count)
    correction = lax.dot_general(
        solved, ends, (((0,), (0,)), ((), ())), precision=HIGH, preferred_element_type=F32
    )
    after_high, after_low = split((sensitivity - correction) * (1.0 / unit)[:, None])

    packed = products(gathered.reshape(blocks, zs * CORES, Y, slots, col_count), after_high, after_low)
    arrived = lax.all_to_all(packed.astype(jnp.float16), "col", 0, 0, tiled=True)
    total = jnp.sum(arrived.astype(F32), axis=0) * unit[None]
    return total.T


def solution(mesh):
    placed = (P("row", "col"), P("col", "row"), P(), P(), P(), P())
    return jax.shard_map(
        on_device, mesh=mesh, in_specs=placed, out_specs=P("row", "col"), check_vma=False
    )
```

```python
import jax
import jax.numpy as jnp
from jax import lax
from jax.experimental import pallas as pl
from jax.experimental.pallas import tpu as pltpu
from jax.sharding import PartitionSpec as P

HIGH = lax.Precision.HIGHEST
F32 = jnp.float32
BF16 = jnp.bfloat16

Y, Z, CORES = 2, 16, 2
COLS = 8
BR = 64


def row_of(y, z, core):
    return y * Z * CORES + z * CORES + core


ROWS = [(y, z, core) for y in range(Y) for z in range(Z) for core in range(CORES)]
OTHER_Y = [(row_of(y, z, k), row_of(1 - y, z, k)) for y, z, k in ROWS]
ALONG_Z_CORE = [[row_of(y, z, k) for z in range(Z) for k in range(CORES)] for y in range(Y)]
ALONG_Z = [[row_of(y, z, k) for z in range(Z)] for y in range(Y) for k in range(CORES)]
OTHER_CORE = [(row_of(y, z, k), row_of(y, z, 1 - k)) for y, z, k in ROWS]


def incidence_of(node_ids, from_node, to_node):
    plus = (node_ids[:, None] == from_node[None, :]).astype(BF16)
    minus = (node_ids[:, None] == to_node[None, :]).astype(BF16)
    return plus - minus


def split(values):
    high = lax.reduce_precision(values, 8, 7)
    return high.astype(BF16), (values - high).astype(BF16)


def in_order(position, mine, other):
    return jnp.where(position == 0, jnp.stack([mine, other]), jnp.stack([other, mine]))


def nt(left, right):
    return lax.dot_general(left, right, (((1,), (1,)), ((), ())), preferred_element_type=F32)


def products(loads, high, low):
    blocks, lines, sides, slots, nodes = loads.shape
    rows = high.shape[0]
    count = lines * slots
    taken = 4

    def body(loads_ref, high_ref, low_ref, out_ref):
        tile = loads_ref[...].reshape(taken * count, nodes)
        out_ref[...] = (nt(tile, high_ref[...]) + nt(tile, low_ref[...])).reshape(taken, count, rows)

    return pl.pallas_call(
        body,
        grid=(sides, blocks // taken),
        in_specs=[
            pl.BlockSpec((taken, lines, 1, slots, nodes), lambda side, block: (block, 0, side, 0, 0)),
            pl.BlockSpec(high.shape, lambda side, block: (0, 0)),
            pl.BlockSpec(low.shape, lambda side, block: (0, 0)),
        ],
        out_specs=pl.BlockSpec((taken, count, rows), lambda side, block: (side * (blocks // taken) + block, 0, 0)),
        out_shape=jax.ShapeDtypeStruct((sides * blocks, count, rows), F32),
        compiler_params=pltpu.CompilerParams(vmem_limit_bytes=48 * 1024 * 1024),
    )(loads, high, low)


def solve(mine, other, reach, parts):
    size, width = BR, parts.shape[1]
    tail = mine.shape[0] - size // 2 - 8
    lanes = 128
    height = size // 2

    def body(mine_ref, other_ref, reach_ref, parts_ref, out_ref, bound_ref):
        sums = mine_ref[tail:] + other_ref[tail:]
        left = jnp.concatenate([sums[:height, :size], sums[:height, size:]], axis=0)
        left = jnp.concatenate([left, jnp.zeros((size, lanes - size), F32)], axis=1)
        rows = lax.broadcasted_iota(jnp.int32, (size, lanes), 0)
        diagonal = rows == lax.broadcasted_iota(jnp.int32, (size, lanes), 1)
        left = left + jnp.where(diagonal, reach_ref[...], 0.0)
        end_bound = jnp.sum(jnp.where(diagonal, sums[height:height + 1], 0.0), axis=1, keepdims=True)
        parts = [left] + [parts_ref[:size, at:at + lanes] for at in range(0, width, lanes)]
        own, other = jnp.zeros((size, lanes), F32), jnp.zeros((size, lanes), F32)
        for k in range(0, size, 2):
            first = jnp.broadcast_to(parts[0][:, k:k + 1], (size, lanes))
            second = jnp.broadcast_to(parts[0][:, k + 1:k + 2], (size, lanes))
            a, b, c, d = first[k:k + 1], second[k:k + 1], first[k + 1:k + 2], second[k + 1:k + 2]
            inverse = 1.0 / (a * d - b * c)
            upper, lower = rows == k, rows == k + 1
            pivots = upper | lower
            up = jnp.where(pivots, 0.0, (first * d - second * c) * inverse)
            down = jnp.where(pivots, 0.0, (second * a - first * b) * inverse)
            own = jnp.where(upper, d * inverse, jnp.where(lower, a * inverse, own))
            other = jnp.where(upper, -b * inverse, jnp.where(lower, -c * inverse, other))
            parts = [values - up * values[k:k + 1] - down * values[k + 1:k + 2] for values in parts]
        even = rows % 2 == 0
        for at, values in enumerate(parts[1:]):
            following = jnp.concatenate([values[1:], values[:1]], axis=0)
            previous = jnp.concatenate([values[-1:], values[:-1]], axis=0)
            solved = own * values + other * jnp.where(even, following, previous)
            here = slice(at * lanes, (at + 1) * lanes)
            out_ref[:, here] = solved
            bound_ref[:, here] = parts_ref[size:, here] + jnp.sum(jnp.abs(solved) * end_bound, axis=0, keepdims=True)

    out_shape = (jax.ShapeDtypeStruct((size, width), F32), jax.ShapeDtypeStruct((8, width), F32))
    return pl.pallas_call(body, out_shape=out_shape)(mine, other, reach, parts)


def on_device(sensitivity, injections, from_node, to_node, switch_flags, impedance):
    row_count, col_count = sensitivity.shape
    row = lax.axis_index("row")
    col = lax.axis_index("col")
    y, core = row // (Z * CORES), row % CORES
    slots = injections.shape[1]

    loads = injections.T
    other_loads = lax.ppermute(loads, "row", OTHER_Y)

    high, low = split(sensitivity)
    col_select = incidence_of(col * col_count + jnp.arange(col_count, dtype=jnp.int32), from_node, to_node)
    row_select = incidence_of(row * row_count + jnp.arange(row_count, dtype=jnp.int32), from_node, to_node)
    part = nt(col_select.T, high) + nt(col_select.T, low)
    reach_of_rows = jnp.sum(jnp.abs(sensitivity), axis=1)
    part = jnp.concatenate([part, jnp.broadcast_to(reach_of_rows[None], (8, row_count))], axis=0)
    copies = jnp.broadcast_to(part[None], (COLS,) + part.shape)
    copies, other_loads = lax.optimization_barrier((copies, other_loads))

    pair = in_order(y, loads, other_loads)
    gathered = lax.all_gather(pair, "row", axis_index_groups=ALONG_Z_CORE, axis=0)

    parts = lax.all_to_all(copies, "col", 0, 0, tiled=True)
    parts = jnp.sum(parts, axis=0)
    columns_t, row_bound = parts[:BR], parts[BR:]

    half = row_count // 2
    first, second = columns_t[:, :half], columns_t[:, half:]
    cap_part = jnp.dot(columns_t, row_select.astype(F32), precision=HIGH, preferred_element_type=F32)
    cap_part = jnp.concatenate([cap_part[: BR // 2], cap_part[BR // 2:]], axis=1)
    end_bound = jnp.dot(row_bound, jnp.abs(row_select.astype(F32)), precision=HIGH, preferred_element_type=F32)
    cap_part = jnp.concatenate([cap_part, jnp.concatenate([end_bound, end_bound], axis=1)], axis=0)
    give = jnp.concatenate([jnp.where(y == 0, second, first), cap_part], axis=0)
    take = lax.ppermute(give, "row", OTHER_Y)
    blocks = COLS // Y
    block = jnp.where(col // blocks == y, jnp.where(y == 0, first, second), take[:BR])
    line = lax.all_gather(
        jnp.concatenate([block, cap_part + take[BR:]], axis=0), "row", axis_index_groups=ALONG_Z, axis=0
    )
    zs = Z // blocks
    ends = lax.dynamic_slice_in_dim(line[:, :BR], (col % blocks) * zs, zs, 0).reshape(zs * BR, half)
    mine = jnp.concatenate([ends, jnp.sum(line[:, BR:], axis=0)], axis=0)
    other = lax.ppermute(mine, "row", OTHER_CORE)
    ends = in_order(core, mine[: zs * BR], other[: zs * BR])
    end_bound = mine[-8, :BR] + other[-8, :BR]
    end_unit = (jnp.maximum(end_bound, 1e-30) / 8192.0)[:, None]
    ends = ends.reshape(CORES, zs, BR, half)
    other_ends = lax.ppermute((ends * (1.0 / end_unit)).astype(jnp.float16), "row", OTHER_Y)

    reach = impedance * (1.0 + 3.0 * switch_flags.astype(F32))
    reach = jnp.concatenate([reach, jnp.zeros_like(reach)])[None]
    solved, bound = solve(mine, other, reach, parts)
    ends = in_order(y, ends, other_ends.astype(F32) * end_unit)
    ends = ends.transpose(3, 2, 1, 0, 4).reshape(BR, col_count)
    correction = lax.dot_general(
        solved, ends, (((0,), (0,)), ((), ())), precision=HIGH, preferred_element_type=F32
    )
    after_high, after_low = split(sensitivity - correction)

    packed = products(gathered.reshape(blocks, zs * CORES, Y, slots, col_count), after_high, after_low)

    unit = jnp.maximum(bound[0], 1e-30) / 8192.0
    arrived = lax.all_to_all((packed * (1.0 / unit)).astype(jnp.float16), "col", 0, 0, tiled=True)
    total = jnp.sum(arrived.astype(F32), axis=0) * unit[None]
    return total.T


def solution(mesh):
    placed = (P("row", "col"), P("col", "row"), P(), P(), P(), P())
    return jax.shard_map(
        on_device, mesh=mesh, in_specs=placed, out_specs=P("row", "col"), check_vma=False
    )
```

```python
import jax
import jax.numpy as jnp
from jax import lax
from jax.experimental import pallas as pl
from jax.experimental.pallas import tpu as pltpu
from jax.sharding import PartitionSpec as P

HIGH = lax.Precision.HIGHEST
F32 = jnp.float32
BF16 = jnp.bfloat16

Y, Z, CORES = 2, 16, 2
COLS = 8
BR = 64


def row_of(y, z, core):
    return y * Z * CORES + z * CORES + core


ROWS = [(y, z, core) for y in range(Y) for z in range(Z) for core in range(CORES)]
OTHER_Y = [(row_of(y, z, k), row_of(1 - y, z, k)) for y, z, k in ROWS]
ALONG_Z_CORE = [[row_of(y, z, k) for z in range(Z) for k in range(CORES)] for y in range(Y)]
ALONG_Y = [[row_of(y, z, k) for y in range(Y)] for z in range(Z) for k in range(CORES)]
ALONG_Z = [[row_of(y, z, k) for z in range(Z)] for y in range(Y) for k in range(CORES)]
OTHER_CORE = [(row_of(y, z, k), row_of(y, z, 1 - k)) for y, z, k in ROWS]


def incidence_of(node_ids, from_node, to_node):
    plus = (node_ids[:, None] == from_node[None, :]).astype(F32)
    minus = (node_ids[:, None] == to_node[None, :]).astype(F32)
    return plus - minus


def split(values):
    high = lax.reduce_precision(values, 8, 7)
    return high.astype(BF16), (values - high).astype(BF16)


def in_order(position, mine, other):
    return jnp.where(position == 0, jnp.stack([mine, other]), jnp.stack([other, mine]))


def nt(left, right):
    return lax.dot_general(left, right, (((1,), (1,)), ((), ())), preferred_element_type=F32)


def differences(sensitivity, ends):
    rows, nodes = sensitivity.shape

    def body(values_ref, ends_ref, out_ref):
        values = values_ref[...]
        high = values.astype(BF16)
        low = (values - high.astype(F32)).astype(BF16)
        branch = lax.broadcasted_iota(jnp.int32, (BR, BR), 0)
        diagonal = branch == lax.broadcasted_iota(jnp.int32, (BR, BR), 1)
        ids = jnp.sum(jnp.where(diagonal, ends_ref[0:1], 0.0), axis=1, keepdims=True)
        other_ids = jnp.sum(jnp.where(diagonal, ends_ref[1:2], 0.0), axis=1, keepdims=True)
        node = lax.broadcasted_iota(jnp.int32, (BR, nodes), 1).astype(F32)
        select = jnp.where(node == ids, 1.0, jnp.where(node == other_ids, -1.0, 0.0)).astype(BF16)
        columns = nt(select, high) + nt(select, low)
        sums = nt(jnp.ones((8, nodes), BF16), jnp.abs(high))
        for copy in range(COLS):
            out_ref[copy, :BR] = columns
            out_ref[copy, BR:] = sums

    return pl.pallas_call(
        body,
        out_shape=jax.ShapeDtypeStruct((COLS, BR + 8, rows), F32),
        compiler_params=pltpu.CompilerParams(vmem_limit_bytes=20 * 1024 * 1024),
    )(sensitivity, ends)


def products(loads, sensitivity, solved, ends, other_ends, y):
    blocks, lines, sides, slots, nodes = loads.shape
    rows = sensitivity.shape[0]
    cores, places, _, half = ends.shape
    count = lines * slots
    taken = 4

    def split_here(values):
        high = values.astype(BF16)
        return high, (values - high.astype(F32)).astype(BF16)

    def body(y_ref, loads_ref, values_ref, solved_ref, ends_ref, other_ref, out_ref, high, low, ends_high, ends_low):
        @pl.when((pl.program_id(0) == 0) & (pl.program_id(1) == 0))
        def _():
            first = y_ref[0] == 0
            for place in range(places):
                for core in range(cores):
                    mine, other = ends_ref[core, place], other_ref[core, place]
                    at = (place * cores + core) * 2 * half
                    for piece in (jnp.where(first, mine, other), jnp.where(first, other, mine)):
                        ends_high[:, at:at + half], ends_low[:, at:at + half] = split_here(piece)
                        at += half
            solved_high, solved_low = split_here(solved_ref[...].T)
            for at in range(0, nodes, 512):
                here = slice(at, at + 512)
                drop = jnp.dot(solved_high, ends_high[:, here], preferred_element_type=F32)
                drop += jnp.dot(solved_high, ends_low[:, here], preferred_element_type=F32)
                drop += jnp.dot(solved_low, ends_high[:, here], preferred_element_type=F32)
                high[:, here], low[:, here] = split_here(values_ref[:, here] - drop)

        tile = loads_ref[...].reshape(taken * count, nodes)
        out_ref[...] = (nt(tile, high[...]) + nt(tile, low[...])).reshape(taken, count, rows)

    def whole(shape):
        return pl.BlockSpec(shape, lambda side, block: (0,) * len(shape))

    return pl.pallas_call(
        body,
        grid=(sides, blocks // taken),
        in_specs=[
            pl.BlockSpec(memory_space=pltpu.SMEM),
            pl.BlockSpec((taken, lines, 1, slots, nodes), lambda side, block: (block, 0, side, 0, 0)),
            whole(sensitivity.shape), whole(solved.shape), whole(ends.shape), whole(ends.shape),
        ],
        out_specs=pl.BlockSpec((taken, count, rows), lambda side, block: (side * (blocks // taken) + block, 0, 0)),
        out_shape=jax.ShapeDtypeStruct((sides * blocks, count, rows), F32),
        scratch_shapes=[pltpu.VMEM((rows, nodes), BF16)] * 2 + [pltpu.VMEM((BR, nodes), BF16)] * 2,
        compiler_params=pltpu.CompilerParams(vmem_limit_bytes=48 * 1024 * 1024),
    )(y.astype(jnp.int32).reshape(1), loads, sensitivity, solved, ends, other_ends)


def unit_of(bound):
    return jnp.maximum(bound, 1e-30) / 8192.0


def solve(mine, other, impedance, flags, parts):
    size, width = BR, parts.shape[1]
    tail = mine.shape[0] - size // 2 - 8
    lanes = 128
    height = size // 2

    def body(mine_ref, other_ref, impedance_ref, flags_ref, parts_ref, out_ref, unit_ref, inverse_ref):
        sums = mine_ref[tail:] + other_ref[tail:]
        left = jnp.concatenate([sums[:height, :size], sums[:height, size:]], axis=0)
        left = jnp.concatenate([left, jnp.zeros((size, lanes - size), F32)], axis=1)
        rows = lax.broadcasted_iota(jnp.int32, (size, lanes), 0)
        diagonal = rows == lax.broadcasted_iota(jnp.int32, (size, lanes), 1)
        reach = impedance_ref[...] * (1.0 + 3.0 * flags_ref[...].astype(F32))
        reach = jnp.concatenate([reach, jnp.zeros_like(reach)], axis=1)
        left = left + jnp.where(diagonal, reach, 0.0)
        end_bound = jnp.sum(jnp.where(diagonal, sums[height:height + 1], 0.0), axis=1, keepdims=True)
        parts = [left] + [parts_ref[:size, at:at + lanes] for at in range(0, width, lanes)]
        own, other = jnp.zeros((size, lanes), F32), jnp.zeros((size, lanes), F32)
        for k in range(0, size, 2):
            first = jnp.broadcast_to(parts[0][:, k:k + 1], (size, lanes))
            second = jnp.broadcast_to(parts[0][:, k + 1:k + 2], (size, lanes))
            a, b, c, d = first[k:k + 1], second[k:k + 1], first[k + 1:k + 2], second[k + 1:k + 2]
            inverse = 1.0 / (a * d - b * c)
            upper, lower = rows == k, rows == k + 1
            pivots = upper | lower
            up = jnp.where(pivots, 0.0, (first * d - second * c) * inverse)
            down = jnp.where(pivots, 0.0, (second * a - first * b) * inverse)
            own = jnp.where(upper, d * inverse, jnp.where(lower, a * inverse, own))
            other = jnp.where(upper, -b * inverse, jnp.where(lower, -c * inverse, other))
            parts = [values - up * values[k:k + 1] - down * values[k + 1:k + 2] for values in parts]
        even = rows % 2 == 0
        for at, values in enumerate(parts[1:]):
            following = jnp.concatenate([values[1:], values[:1]], axis=0)
            previous = jnp.concatenate([values[-1:], values[:-1]], axis=0)
            solved = own * values + other * jnp.where(even, following, previous)
            here = slice(at * lanes, (at + 1) * lanes)
            out_ref[:, here] = solved * unit_of(end_bound)
            bound = parts_ref[size:size + 1, here] + jnp.sum(jnp.abs(solved) * end_bound, axis=0, keepdims=True)
            unit_ref[:, here] = unit_of(bound)
            inverse_ref[:, here] = 1.0 / unit_of(bound)

    out_shape = tuple(jax.ShapeDtypeStruct((height, width), F32) for height in (size, 1, 1))
    return pl.pallas_call(body, out_shape=out_shape)(mine, other, impedance, flags, parts)


def on_device(sensitivity, injections, from_node, to_node, switch_flags, impedance):
    row_count, col_count = sensitivity.shape
    row = lax.axis_index("row")
    col = lax.axis_index("col")
    y, core = row // (Z * CORES), row % CORES
    slots = injections.shape[1]

    loads = injections.T
    pair = lax.all_gather(loads, "row", axis_index_groups=ALONG_Y, axis=0)

    row_select = incidence_of(row * row_count + jnp.arange(row_count, dtype=jnp.int32), from_node, to_node)
    copies = differences(sensitivity, (jnp.stack([from_node, to_node]) - col * col_count).astype(F32))

    gathered = lax.all_gather(pair, "row", axis_index_groups=ALONG_Z_CORE, axis=0)

    parts = lax.all_to_all(copies, "col", 0, 0, tiled=True)
    parts = jnp.sum(parts, axis=0)
    columns_t, row_bound = parts[:BR], parts[BR:]

    half = row_count // 2
    first, second = columns_t[:, :half], columns_t[:, half:]
    cap_part = jnp.dot(columns_t, row_select, precision=HIGH, preferred_element_type=F32)
    cap_part = jnp.concatenate([cap_part[: BR // 2], cap_part[BR // 2:]], axis=1)
    end_bound = jnp.dot(row_bound, jnp.abs(row_select), precision=HIGH, preferred_element_type=F32)
    cap_part = jnp.concatenate([cap_part, jnp.concatenate([end_bound, end_bound], axis=1)], axis=0)
    give = jnp.concatenate([jnp.where(y == 0, second, first), cap_part], axis=0)
    take = lax.ppermute(give, "row", OTHER_Y)
    blocks = COLS // Y
    block = jnp.where(col // blocks == y, jnp.where(y == 0, first, second), take[:BR])
    line = lax.all_gather(
        jnp.concatenate([block, cap_part + take[BR:]], axis=0), "row", axis_index_groups=ALONG_Z, axis=0
    )
    zs = Z // blocks
    ends = lax.dynamic_slice_in_dim(line[:, :BR], (col % blocks) * zs, zs, 0).reshape(zs * BR, half)
    mine = jnp.concatenate([ends, jnp.sum(line[:, BR:], axis=0)], axis=0)
    other = lax.ppermute(mine, "row", OTHER_CORE)
    ends = in_order(core, mine[: zs * BR], other[: zs * BR])
    end_bound = mine[-8, :BR] + other[-8, :BR]
    ends = ends.reshape(CORES, zs, BR, half) * (1.0 / unit_of(end_bound))[:, None]
    other_ends = lax.ppermute(ends.astype(jnp.float16), "row", OTHER_Y)

    solved, unit, inverse = solve(mine, other, impedance[None], switch_flags[None], parts)

    loads = gathered.reshape(blocks, zs * CORES, Y, slots, col_count)
    packed = products(loads, sensitivity, solved, ends, other_ends.astype(F32), y)

    arrived = lax.all_to_all((packed * inverse).astype(jnp.float16), "col", 0, 0, tiled=True)
    total = jnp.sum(arrived.astype(F32), axis=0) * unit
    return total.T


def solution(mesh):
    placed = (P("row", "col"), P("col", "row"), P(), P(), P(), P())
    return jax.shard_map(
        on_device, mesh=mesh, in_specs=placed, out_specs=P("row", "col"), check_vma=False
    )
```

```python
import jax
import jax.numpy as jnp
from jax import lax
from jax.experimental import pallas as pl
from jax.experimental.pallas import tpu as pltpu
from jax.sharding import PartitionSpec as P

HIGH = lax.Precision.HIGHEST
F32 = jnp.float32
BF16 = jnp.bfloat16

Y, Z, CORES = 2, 16, 2
COLS = 8
BR = 64


def row_of(y, z, core):
    return y * Z * CORES + z * CORES + core


ROWS = [(y, z, core) for y in range(Y) for z in range(Z) for core in range(CORES)]
OTHER_Y = [(row_of(y, z, k), row_of(1 - y, z, k)) for y, z, k in ROWS]
ALONG_Z_CORE = [[row_of(y, z, k) for z in range(Z) for k in range(CORES)] for y in range(Y)]
ALONG_Y = [[row_of(y, z, k) for y in range(Y)] for z in range(Z) for k in range(CORES)]
ALONG_Z = [[row_of(y, z, k) for z in range(Z)] for y in range(Y) for k in range(CORES)]
OTHER_CORE = [(row_of(y, z, k), row_of(y, z, 1 - k)) for y, z, k in ROWS]


def incidence_of(node_ids, from_node, to_node):
    plus = (node_ids[:, None] == from_node[None, :]).astype(F32)
    minus = (node_ids[:, None] == to_node[None, :]).astype(F32)
    return plus - minus


def split(values):
    high = lax.reduce_precision(values, 8, 7)
    return high.astype(BF16), (values - high).astype(BF16)


def in_order(position, mine, other):
    return jnp.where(position == 0, jnp.stack([mine, other]), jnp.stack([other, mine]))


def nt(left, right):
    return lax.dot_general(left, right, (((1,), (1,)), ((), ())), preferred_element_type=F32)


def differences(sensitivity, ends):
    rows, nodes = sensitivity.shape

    def body(values_ref, ends_ref, out_ref):
        values = values_ref[...]
        high = values.astype(BF16)
        low = (values - high.astype(F32)).astype(BF16)
        branch = lax.broadcasted_iota(jnp.int32, (BR, BR), 0)
        diagonal = branch == lax.broadcasted_iota(jnp.int32, (BR, BR), 1)
        ids = jnp.sum(jnp.where(diagonal, ends_ref[0:1], 0.0), axis=1, keepdims=True)
        other_ids = jnp.sum(jnp.where(diagonal, ends_ref[1:2], 0.0), axis=1, keepdims=True)
        node = lax.broadcasted_iota(jnp.int32, (BR, nodes), 1).astype(F32)
        select = jnp.where(node == ids, 1.0, jnp.where(node == other_ids, -1.0, 0.0)).astype(BF16)
        columns = nt(select, high) + nt(select, low)
        sums = nt(jnp.ones((8, nodes), BF16), jnp.abs(high))
        for copy in range(COLS):
            out_ref[copy, :BR] = columns
            out_ref[copy, BR:] = sums

    return pl.pallas_call(
        body,
        out_shape=jax.ShapeDtypeStruct((COLS, BR + 8, rows), F32),
        compiler_params=pltpu.CompilerParams(vmem_limit_bytes=20 * 1024 * 1024),
    )(sensitivity, ends)


def products(loads, sensitivity, solved, ends, other_ends, unit, y):
    blocks, lines, sides, slots, nodes = loads.shape
    rows = sensitivity.shape[0]
    cores, places, _, half = ends.shape
    count = lines * slots
    taken = 4

    def split_here(values):
        high = values.astype(BF16)
        return high, (values - high.astype(F32)).astype(BF16)

    def body(y_ref, loads_ref, values_ref, solved_ref, ends_ref, other_ref, unit_ref, out_ref, units_ref, both, inverse, ends_high, ends_low):
        @pl.when((pl.program_id(0) == 0) & (pl.program_id(1) == 0))
        def _():
            first = y_ref[0] == 0
            for place in range(places):
                for core in range(cores):
                    mine, other = ends_ref[core, place], other_ref[core, place]
                    at = (place * cores + core) * 2 * half
                    for piece in (jnp.where(first, mine, other), jnp.where(first, other, mine)):
                        ends_high[:, at:at + half], ends_low[:, at:at + half] = split_here(piece)
                        at += half
            solved_high, solved_low = split_here(solved_ref[...].T)
            for at in range(0, nodes, 512):
                here = slice(at, at + 512)
                drop = jnp.dot(solved_high, ends_high[:, here], preferred_element_type=F32)
                drop += jnp.dot(solved_high, ends_low[:, here], preferred_element_type=F32)
                drop += jnp.dot(solved_low, ends_high[:, here], preferred_element_type=F32)
                both[:rows, here], both[rows:, here] = split_here(values_ref[:, here] - drop)
            units_ref[...] = jnp.broadcast_to(unit_ref[...], (count, rows)).T
            inverse[...] = 1.0 / units_ref[...]

        tile = loads_ref[...].reshape(taken * count, nodes)
        sums = nt(both[...], tile)
        sums = sums[:rows] + sums[rows:]
        for block in range(taken):
            out_ref[block] = sums[:, block * count:(block + 1) * count] * inverse[...]

    def whole(shape):
        return pl.BlockSpec(shape, lambda side, block: (0,) * len(shape))

    return pl.pallas_call(
        body,
        grid=(sides, blocks // taken),
        in_specs=[
            pl.BlockSpec(memory_space=pltpu.SMEM),
            pl.BlockSpec((taken, lines, 1, slots, nodes), lambda side, block: (block, 0, side, 0, 0)),
            whole(sensitivity.shape), whole(solved.shape), whole(ends.shape), whole(ends.shape), whole(unit.shape),
        ],
        out_specs=(
            pl.BlockSpec((taken, rows, count), lambda side, block: (side * (blocks // taken) + block, 0, 0)),
            whole((rows, count)),
        ),
        out_shape=(
            jax.ShapeDtypeStruct((sides * blocks, rows, count), F32), jax.ShapeDtypeStruct((rows, count), F32)
        ),
        scratch_shapes=[
            pltpu.VMEM((2 * rows, nodes), BF16), pltpu.VMEM((rows, count), F32),
            pltpu.VMEM((BR, nodes), BF16), pltpu.VMEM((BR, nodes), BF16),
        ],
        compiler_params=pltpu.CompilerParams(vmem_limit_bytes=48 * 1024 * 1024),
    )(y.astype(jnp.int32).reshape(1), loads, sensitivity, solved, ends, other_ends, unit)


def unit_of(bound):
    return jnp.maximum(bound, 1e-30) / 8192.0


def solve(mine, other, impedance, flags, parts):
    size, width = BR, parts.shape[1]
    tail = mine.shape[0] - size // 2 - 8
    lanes = 128
    height = size // 2

    def body(mine_ref, other_ref, impedance_ref, flags_ref, parts_ref, out_ref, unit_ref):
        sums = mine_ref[tail:] + other_ref[tail:]
        left = jnp.concatenate([sums[:height, :size], sums[:height, size:]], axis=0)
        left = jnp.concatenate([left, jnp.zeros((size, lanes - size), F32)], axis=1)
        rows = lax.broadcasted_iota(jnp.int32, (size, lanes), 0)
        diagonal = rows == lax.broadcasted_iota(jnp.int32, (size, lanes), 1)
        reach = impedance_ref[...] * (1.0 + 3.0 * flags_ref[...].astype(F32))
        reach = jnp.concatenate([reach, jnp.zeros_like(reach)], axis=1)
        left = left + jnp.where(diagonal, reach, 0.0)
        end_bound = jnp.sum(jnp.where(diagonal, sums[height:height + 1], 0.0), axis=1, keepdims=True)
        parts = [left] + [parts_ref[:size, at:at + lanes] for at in range(0, width, lanes)]
        own, other = jnp.zeros((size, lanes), F32), jnp.zeros((size, lanes), F32)
        for k in range(0, size, 2):
            first = jnp.broadcast_to(parts[0][:, k:k + 1], (size, lanes))
            second = jnp.broadcast_to(parts[0][:, k + 1:k + 2], (size, lanes))
            a, b, c, d = first[k:k + 1], second[k:k + 1], first[k + 1:k + 2], second[k + 1:k + 2]
            inverse = 1.0 / (a * d - b * c)
            upper, lower = rows == k, rows == k + 1
            pivots = upper | lower
            up = jnp.where(pivots, 0.0, (first * d - second * c) * inverse)
            down = jnp.where(pivots, 0.0, (second * a - first * b) * inverse)
            own = jnp.where(upper, d * inverse, jnp.where(lower, a * inverse, own))
            other = jnp.where(upper, -b * inverse, jnp.where(lower, -c * inverse, other))
            parts = [values - up * values[k:k + 1] - down * values[k + 1:k + 2] for values in parts]
        even = rows % 2 == 0
        for at, values in enumerate(parts[1:]):
            following = jnp.concatenate([values[1:], values[:1]], axis=0)
            previous = jnp.concatenate([values[-1:], values[:-1]], axis=0)
            solved = own * values + other * jnp.where(even, following, previous)
            here = slice(at * lanes, (at + 1) * lanes)
            out_ref[:, here] = solved * unit_of(end_bound)
            bound = parts_ref[size:size + 1, here] + jnp.sum(jnp.abs(solved) * end_bound, axis=0, keepdims=True)
            unit_ref[:, here] = unit_of(bound)

    out_shape = tuple(jax.ShapeDtypeStruct((height, width), F32) for height in (size, 1))
    params = pltpu.CompilerParams(vmem_limit_bytes=8 * 1024 * 1024)
    return pl.pallas_call(body, out_shape=out_shape, compiler_params=params)(mine, other, impedance, flags, parts)


def on_device(sensitivity, injections, from_node, to_node, switch_flags, impedance):
    row_count, col_count = sensitivity.shape
    row = lax.axis_index("row")
    col = lax.axis_index("col")
    y, core = row // (Z * CORES), row % CORES
    slots = injections.shape[1]

    loads = injections.T
    pair = lax.all_gather(loads, "row", axis_index_groups=ALONG_Y, axis=0)

    row_select = incidence_of(row * row_count + jnp.arange(row_count, dtype=jnp.int32), from_node, to_node)
    copies = differences(sensitivity, (jnp.stack([from_node, to_node]) - col * col_count).astype(F32))

    gathered = lax.all_gather(pair, "row", axis_index_groups=ALONG_Z_CORE, axis=0)

    parts = lax.all_to_all(copies, "col", 0, 0, tiled=True)
    parts = jnp.sum(parts, axis=0)
    columns_t, row_bound = parts[:BR], parts[BR:]

    half = row_count // 2
    first, second = columns_t[:, :half], columns_t[:, half:]
    cap_part = jnp.dot(columns_t, row_select, precision=HIGH, preferred_element_type=F32)
    cap_part = jnp.concatenate([cap_part[: BR // 2], cap_part[BR // 2:]], axis=1)
    end_bound = jnp.dot(row_bound, jnp.abs(row_select), precision=HIGH, preferred_element_type=F32)
    cap_part = jnp.concatenate([cap_part, jnp.concatenate([end_bound, end_bound], axis=1)], axis=0)
    give = jnp.concatenate([jnp.where(y == 0, second, first), cap_part], axis=0)
    take = lax.ppermute(give, "row", OTHER_Y)
    blocks = COLS // Y
    block = jnp.where(col // blocks == y, jnp.where(y == 0, first, second), take[:BR])
    line = lax.all_gather(
        jnp.concatenate([block, cap_part + take[BR:]], axis=0), "row", axis_index_groups=ALONG_Z, axis=0
    )
    zs = Z // blocks
    ends = lax.dynamic_slice_in_dim(line[:, :BR], (col % blocks) * zs, zs, 0).reshape(zs * BR, half)
    mine = jnp.concatenate([ends, jnp.sum(line[:, BR:], axis=0)], axis=0)
    other = lax.ppermute(mine, "row", OTHER_CORE)
    ends = in_order(core, mine[: zs * BR], other[: zs * BR])
    end_bound = mine[-8, :BR] + other[-8, :BR]
    ends = ends.reshape(CORES, zs, BR, half) * (1.0 / unit_of(end_bound))[:, None]
    other_ends = lax.ppermute(ends.astype(jnp.float16), "row", OTHER_Y)

    solved, unit = solve(mine, other, impedance[None], switch_flags[None], parts)

    loads = gathered.reshape(blocks, zs * CORES, Y, slots, col_count)
    packed, units = products(loads, sensitivity, solved, ends, other_ends.astype(F32), unit, y)

    arrived = lax.all_to_all(packed.astype(jnp.float16), "col", 0, 0, tiled=True)
    total = jnp.sum(arrived.astype(F32), axis=0) * units
    return total


def solution(mesh):
    placed = (P("row", "col"), P("col", "row"), P(), P(), P(), P())
    return jax.shard_map(
        on_device, mesh=mesh, in_specs=placed, out_specs=P("row", "col"), check_vma=False
    )
```

```python
import jax
import jax.numpy as jnp
from jax import lax
from jax.experimental import pallas as pl
from jax.experimental.pallas import tpu as pltpu
from jax.sharding import PartitionSpec as P

HIGH = lax.Precision.HIGHEST
F32 = jnp.float32
BF16 = jnp.bfloat16

Y, Z, CORES = 2, 16, 2
COLS = 8
BR = 64


def row_of(y, z, core):
    return y * Z * CORES + z * CORES + core


ROWS = [(y, z, core) for y in range(Y) for z in range(Z) for core in range(CORES)]
OTHER_Y = [(row_of(y, z, k), row_of(1 - y, z, k)) for y, z, k in ROWS]
ALONG_Z_CORE = [[row_of(y, z, k) for z in range(Z) for k in range(CORES)] for y in range(Y)]
ALONG_Y = [[row_of(y, z, k) for y in range(Y)] for z in range(Z) for k in range(CORES)]
ALONG_Z = [[row_of(y, z, k) for z in range(Z)] for y in range(Y) for k in range(CORES)]
OTHER_CORE = [(row_of(y, z, k), row_of(y, z, 1 - k)) for y, z, k in ROWS]


def incidence_of(node_ids, from_node, to_node):
    plus = (node_ids[:, None] == from_node[None, :]).astype(F32)
    minus = (node_ids[:, None] == to_node[None, :]).astype(F32)
    return plus - minus


def split(values):
    high = lax.reduce_precision(values, 8, 7)
    return high.astype(BF16), (values - high).astype(BF16)


def in_order(position, mine, other):
    return jnp.where(position == 0, jnp.stack([mine, other]), jnp.stack([other, mine]))


def nt(left, right):
    return lax.dot_general(left, right, (((1,), (1,)), ((), ())), preferred_element_type=F32)


def differences(sensitivity, ends):
    rows, nodes = sensitivity.shape

    def body(values_ref, ends_ref, out_ref):
        values = values_ref[...]
        high = values.astype(BF16)
        low = (values - high.astype(F32)).astype(BF16)
        branch = lax.broadcasted_iota(jnp.int32, (BR, BR), 0)
        diagonal = branch == lax.broadcasted_iota(jnp.int32, (BR, BR), 1)
        ids = jnp.sum(jnp.where(diagonal, ends_ref[0:1], 0.0), axis=1, keepdims=True)
        other_ids = jnp.sum(jnp.where(diagonal, ends_ref[1:2], 0.0), axis=1, keepdims=True)
        node = lax.broadcasted_iota(jnp.int32, (BR, nodes), 1).astype(F32)
        select = jnp.where(node == ids, 1.0, jnp.where(node == other_ids, -1.0, 0.0)).astype(BF16)
        columns = nt(select, high) + nt(select, low)
        sums = nt(jnp.ones((8, nodes), BF16), jnp.abs(high))
        for copy in range(COLS):
            out_ref[copy, :BR] = columns
            out_ref[copy, BR:] = sums

    return pl.pallas_call(
        body,
        out_shape=jax.ShapeDtypeStruct((COLS, BR + 8, rows), F32),
        compiler_params=pltpu.CompilerParams(vmem_limit_bytes=20 * 1024 * 1024),
    )(sensitivity, ends)


def products(loads, sensitivity, solved, ends, other_ends, unit, y):
    blocks, lines, sides, slots, nodes = loads.shape
    rows = sensitivity.shape[0]
    cores, places, _, half = ends.shape
    count = lines * slots
    taken = 4

    def split_here(values):
        high = values.astype(BF16)
        return high, (values - high.astype(F32)).astype(BF16)

    def body(y_ref, loads_ref, values_ref, solved_ref, ends_ref, other_ref, unit_ref, out_ref, units_ref, both, inverse, ends_high, ends_low):
        @pl.when((pl.program_id(0) == 0) & (pl.program_id(1) == 0))
        def _():
            first = y_ref[0] == 0
            for place in range(places):
                for core in range(cores):
                    mine, other = ends_ref[core, place], other_ref[core, place]
                    at = (place * cores + core) * 2 * half
                    for piece in (jnp.where(first, mine, other), jnp.where(first, other, mine)):
                        ends_high[:, at:at + half], ends_low[:, at:at + half] = split_here(piece)
                        at += half
            solved_high, solved_low = split_here(solved_ref[...].T)
            for at in range(0, nodes, 512):
                here = slice(at, at + 512)
                drop = jnp.dot(solved_high, ends_high[:, here], preferred_element_type=F32)
                drop += jnp.dot(solved_high, ends_low[:, here], preferred_element_type=F32)
                drop += jnp.dot(solved_low, ends_high[:, here], preferred_element_type=F32)
                both[:rows, here], both[rows:, here] = split_here(values_ref[:, here] - drop)
            units_ref[...] = jnp.broadcast_to(unit_ref[...], (count, rows)).T
            inverse[...] = 1.0 / units_ref[...]

        tile = loads_ref[...].reshape(taken * count, nodes)
        sums = nt(both[...], tile)
        sums = sums[:rows] + sums[rows:]
        for block in range(taken):
            out_ref[block] = sums[:, block * count:(block + 1) * count] * inverse[...]

    whole = pl.BlockSpec(memory_space=pltpu.VMEM)

    return pl.pallas_call(
        body,
        grid=(sides, blocks // taken),
        in_specs=[
            pl.BlockSpec(memory_space=pltpu.SMEM),
            pl.BlockSpec((taken, lines, 1, slots, nodes), lambda side, block: (block, 0, side, 0, 0)),
            whole, whole, whole, whole, whole,
        ],
        out_specs=(
            pl.BlockSpec((taken, rows, count), lambda side, block: (side * (blocks // taken) + block, 0, 0)),
            whole,
        ),
        out_shape=(
            jax.ShapeDtypeStruct((sides * blocks, rows, count), F32), jax.ShapeDtypeStruct((rows, count), F32)
        ),
        scratch_shapes=[
            pltpu.VMEM((2 * rows, nodes), BF16), pltpu.VMEM((rows, count), F32),
            pltpu.VMEM((BR, nodes), BF16), pltpu.VMEM((BR, nodes), BF16),
        ],
        compiler_params=pltpu.CompilerParams(vmem_limit_bytes=48 * 1024 * 1024),
    )(y.astype(jnp.int32).reshape(1), loads, sensitivity, solved, ends, other_ends, unit)


def unit_of(bound):
    return jnp.maximum(bound, 1e-30) / 8192.0


def solve(mine, other, impedance, flags, parts):
    size, width = BR, parts.shape[1]
    tail = mine.shape[0] - size // 2 - 8
    lanes = 128
    height = size // 2

    def body(mine_ref, other_ref, impedance_ref, flags_ref, parts_ref, out_ref, unit_ref):
        sums = mine_ref[tail:] + other_ref[tail:]
        left = jnp.concatenate([sums[:height, :size], sums[:height, size:]], axis=0)
        left = jnp.concatenate([left, jnp.zeros((size, lanes - size), F32)], axis=1)
        rows = lax.broadcasted_iota(jnp.int32, (size, lanes), 0)
        diagonal = rows == lax.broadcasted_iota(jnp.int32, (size, lanes), 1)
        reach = impedance_ref[...] * (1.0 + 3.0 * flags_ref[...].astype(F32))
        reach = jnp.concatenate([reach, jnp.zeros_like(reach)], axis=1)
        left = left + jnp.where(diagonal, reach, 0.0)
        end_bound = jnp.sum(jnp.where(diagonal, sums[height:height + 1], 0.0), axis=1, keepdims=True)
        parts = [left] + [parts_ref[:size, at:at + lanes] for at in range(0, width, lanes)]
        own, other = jnp.zeros((size, lanes), F32), jnp.zeros((size, lanes), F32)
        for k in range(0, size, 2):
            first = jnp.broadcast_to(parts[0][:, k:k + 1], (size, lanes))
            second = jnp.broadcast_to(parts[0][:, k + 1:k + 2], (size, lanes))
            a, b, c, d = first[k:k + 1], second[k:k + 1], first[k + 1:k + 2], second[k + 1:k + 2]
            inverse = 1.0 / (a * d - b * c)
            upper, lower = rows == k, rows == k + 1
            pivots = upper | lower
            up = jnp.where(pivots, 0.0, (first * d - second * c) * inverse)
            down = jnp.where(pivots, 0.0, (second * a - first * b) * inverse)
            own = jnp.where(upper, d * inverse, jnp.where(lower, a * inverse, own))
            other = jnp.where(upper, -b * inverse, jnp.where(lower, -c * inverse, other))
            parts = [values - up * values[k:k + 1] - down * values[k + 1:k + 2] for values in parts]
        even = rows % 2 == 0
        for at, values in enumerate(parts[1:]):
            following = jnp.concatenate([values[1:], values[:1]], axis=0)
            previous = jnp.concatenate([values[-1:], values[:-1]], axis=0)
            solved = own * values + other * jnp.where(even, following, previous)
            here = slice(at * lanes, (at + 1) * lanes)
            out_ref[:, here] = solved * unit_of(end_bound)
            bound = parts_ref[size:size + 1, here] + jnp.sum(jnp.abs(solved) * end_bound, axis=0, keepdims=True)
            unit_ref[:, here] = unit_of(bound)

    out_shape = tuple(jax.ShapeDtypeStruct((height, width), F32) for height in (size, 1))
    params = pltpu.CompilerParams(vmem_limit_bytes=8 * 1024 * 1024)
    return pl.pallas_call(body, out_shape=out_shape, compiler_params=params)(mine, other, impedance, flags, parts)


def on_device(sensitivity, injections, from_node, to_node, switch_flags, impedance):
    row_count, col_count = sensitivity.shape
    row = lax.axis_index("row")
    col = lax.axis_index("col")
    y, core = row // (Z * CORES), row % CORES
    slots = injections.shape[1]

    loads = injections.T
    pair = lax.all_gather(loads, "row", axis_index_groups=ALONG_Y, axis=0)

    row_select = incidence_of(row * row_count + jnp.arange(row_count, dtype=jnp.int32), from_node, to_node)
    copies = differences(sensitivity, (jnp.stack([from_node, to_node]) - col * col_count).astype(F32))

    gathered = lax.all_gather(pair, "row", axis_index_groups=ALONG_Z_CORE, axis=0)

    parts = lax.all_to_all(copies, "col", 0, 0, tiled=True)
    parts = jnp.sum(parts, axis=0)
    columns_t, row_bound = parts[:BR], parts[BR:]

    half = row_count // 2
    first, second = columns_t[:, :half], columns_t[:, half:]
    cap_part = jnp.dot(columns_t, row_select, precision=HIGH, preferred_element_type=F32)
    cap_part = jnp.concatenate([cap_part[: BR // 2], cap_part[BR // 2:]], axis=1)
    end_bound = jnp.dot(row_bound, jnp.abs(row_select), precision=HIGH, preferred_element_type=F32)
    cap_part = jnp.concatenate([cap_part, jnp.concatenate([end_bound, end_bound], axis=1)], axis=0)
    give = jnp.concatenate([jnp.where(y == 0, second, first), cap_part], axis=0)
    take = lax.ppermute(give, "row", OTHER_Y)
    blocks = COLS // Y
    block = jnp.where(col // blocks == y, jnp.where(y == 0, first, second), take[:BR])
    line = lax.all_gather(
        jnp.concatenate([block, cap_part + take[BR:]], axis=0), "row", axis_index_groups=ALONG_Z, axis=0
    )
    zs = Z // blocks
    ends = lax.dynamic_slice_in_dim(line[:, :BR], (col % blocks) * zs, zs, 0).reshape(zs * BR, half)
    mine = jnp.concatenate([ends, jnp.sum(line[:, BR:], axis=0)], axis=0)
    other = lax.ppermute(mine, "row", OTHER_CORE)
    ends = in_order(core, mine[: zs * BR], other[: zs * BR])
    end_bound = mine[-8, :BR] + other[-8, :BR]
    ends = ends.reshape(CORES, zs, BR, half) * (1.0 / unit_of(end_bound))[:, None]
    other_ends = lax.ppermute(ends.astype(jnp.float16), "row", OTHER_Y)

    solved, unit = solve(mine, other, impedance[None], switch_flags[None], parts)

    loads = gathered.reshape(blocks, zs * CORES, Y, slots, col_count)
    packed, units = products(loads, sensitivity, solved, ends, other_ends.astype(F32), unit, y)

    arrived = lax.all_to_all(packed.astype(jnp.float16), "col", 0, 0, tiled=True)
    total = jnp.sum(arrived.astype(F32), axis=0) * units
    return total


def solution(mesh):
    placed = (P("row", "col"), P("col", "row"), P(), P(), P(), P())
    return jax.shard_map(
        on_device, mesh=mesh, in_specs=placed, out_specs=P("row", "col"), check_vma=False
    )
```

```python
import jax
import jax.numpy as jnp
from jax import lax
from jax.experimental import pallas as pl
from jax.experimental.pallas import tpu as pltpu
from jax.sharding import PartitionSpec as P

HIGH = lax.Precision.HIGHEST
F32 = jnp.float32
BF16 = jnp.bfloat16

Y, Z, CORES = 2, 16, 2
COLS = 8
BR = 64


def row_of(y, z, core):
    return y * Z * CORES + z * CORES + core


ROWS = [(y, z, core) for y in range(Y) for z in range(Z) for core in range(CORES)]
OTHER_Y = [(row_of(y, z, k), row_of(1 - y, z, k)) for y, z, k in ROWS]
ALONG_Z_CORE = [[row_of(y, z, k) for z in range(Z) for k in range(CORES)] for y in range(Y)]
ALONG_Y = [[row_of(y, z, k) for y in range(Y)] for z in range(Z) for k in range(CORES)]
ALONG_Z = [[row_of(y, z, k) for z in range(Z)] for y in range(Y) for k in range(CORES)]
OTHER_CORE = [(row_of(y, z, k), row_of(y, z, 1 - k)) for y, z, k in ROWS]


def incidence_of(node_ids, from_node, to_node):
    plus = (node_ids[:, None] == from_node[None, :]).astype(F32)
    minus = (node_ids[:, None] == to_node[None, :]).astype(F32)
    return plus - minus


def split(values):
    high = lax.reduce_precision(values, 8, 7)
    return high.astype(BF16), (values - high).astype(BF16)


def in_order(position, mine, other):
    return jnp.where(position == 0, jnp.stack([mine, other]), jnp.stack([other, mine]))


def nt(left, right):
    return lax.dot_general(left, right, (((1,), (1,)), ((), ())), preferred_element_type=F32)


def differences(sensitivity, ends):
    rows, nodes = sensitivity.shape

    def body(values_ref, ends_ref, out_ref):
        values = values_ref[...]
        high = values.astype(BF16)
        low = (values - high.astype(F32)).astype(BF16)
        branch = lax.broadcasted_iota(jnp.int32, (BR, BR), 0)
        diagonal = branch == lax.broadcasted_iota(jnp.int32, (BR, BR), 1)
        ids = jnp.sum(jnp.where(diagonal, ends_ref[0:1], 0.0), axis=1, keepdims=True)
        other_ids = jnp.sum(jnp.where(diagonal, ends_ref[1:2], 0.0), axis=1, keepdims=True)
        node = lax.broadcasted_iota(jnp.int32, (BR, nodes), 1).astype(F32)
        select = jnp.where(node == ids, 1.0, jnp.where(node == other_ids, -1.0, 0.0)).astype(BF16)
        columns = nt(select, high) + nt(select, low)
        sums = nt(jnp.ones((8, nodes), BF16), jnp.abs(high))
        for copy in range(COLS):
            out_ref[copy, :BR] = columns
            out_ref[copy, BR:] = sums

    return pl.pallas_call(
        body,
        out_shape=jax.ShapeDtypeStruct((COLS, BR + 8, rows), F32),
        compiler_params=pltpu.CompilerParams(vmem_limit_bytes=20 * 1024 * 1024),
    )(sensitivity, ends)


def products(loads, sensitivity, solved, ends, other_ends, unit, y):
    blocks, lines, sides, slots, nodes = loads.shape
    rows = sensitivity.shape[0]
    cores, places, _, half = ends.shape
    count = lines * slots
    taken = 4

    def split_here(values):
        high = values.astype(BF16)
        return high, (values - high.astype(F32)).astype(BF16)

    def body(y_ref, loads_ref, values_ref, solved_ref, ends_ref, other_ref, unit_ref, out_ref, units_ref, both, inverse, stacked):
        @pl.when((pl.program_id(0) == 0) & (pl.program_id(1) == 0))
        def _():
            first = y_ref[0] == 0
            for place in range(places):
                for core in range(cores):
                    mine, other = ends_ref[core, place], other_ref[core, place]
                    at = (place * cores + core) * 2 * half
                    for piece in (jnp.where(first, mine, other), jnp.where(first, other, mine)):
                        high, low = split_here(piece)
                        stacked[:BR, at:at + half] = high
                        stacked[BR:2 * BR, at:at + half] = low
                        stacked[2 * BR:, at:at + half] = high
                        at += half
            solved_high, solved_low = split_here(solved_ref[...].T)
            solved_parts = jnp.concatenate([solved_high, solved_high, solved_low], axis=1)
            for at in range(0, nodes, 512):
                here = slice(at, at + 512)
                drop = jnp.dot(solved_parts, stacked[:, here], preferred_element_type=F32)
                both[:rows, here], both[rows:, here] = split_here(values_ref[:, here] - drop)
            units_ref[...] = jnp.broadcast_to(unit_ref[...], (count, rows)).T
            inverse[...] = 1.0 / units_ref[...]

        tile = loads_ref[...].reshape(taken * count, nodes)
        sums = nt(both[...], tile)
        sums = sums[:rows] + sums[rows:]
        for block in range(taken):
            out_ref[block] = sums[:, block * count:(block + 1) * count] * inverse[...]

    whole = pl.BlockSpec(memory_space=pltpu.VMEM)

    return pl.pallas_call(
        body,
        grid=(sides, blocks // taken),
        in_specs=[
            pl.BlockSpec(memory_space=pltpu.SMEM),
            pl.BlockSpec((taken, lines, 1, slots, nodes), lambda side, block: (block, 0, side, 0, 0)),
            whole, whole, whole, whole, whole,
        ],
        out_specs=(
            pl.BlockSpec((taken, rows, count), lambda side, block: (side * (blocks // taken) + block, 0, 0)),
            whole,
        ),
        out_shape=(
            jax.ShapeDtypeStruct((sides * blocks, rows, count), F32), jax.ShapeDtypeStruct((rows, count), F32)
        ),
        scratch_shapes=[
            pltpu.VMEM((2 * rows, nodes), BF16), pltpu.VMEM((rows, count), F32),
            pltpu.VMEM((3 * BR, nodes), BF16),
        ],
        compiler_params=pltpu.CompilerParams(vmem_limit_bytes=48 * 1024 * 1024),
    )(y.astype(jnp.int32).reshape(1), loads, sensitivity, solved, ends, other_ends, unit)


def unit_of(bound):
    return jnp.maximum(bound, 1e-30) / 8192.0


def solve(mine, other, impedance, flags, parts):
    size, width = BR, parts.shape[1]
    tail = mine.shape[0] - size // 2 - 8
    lanes = 128
    height = size // 2

    def body(mine_ref, other_ref, impedance_ref, flags_ref, parts_ref, out_ref, unit_ref):
        sums = mine_ref[tail:] + other_ref[tail:]
        left = jnp.concatenate([sums[:height, :size], sums[:height, size:]], axis=0)
        left = jnp.concatenate([left, jnp.zeros((size, lanes - size), F32)], axis=1)
        rows = lax.broadcasted_iota(jnp.int32, (size, lanes), 0)
        diagonal = rows == lax.broadcasted_iota(jnp.int32, (size, lanes), 1)
        reach = impedance_ref[...] * (1.0 + 3.0 * flags_ref[...].astype(F32))
        reach = jnp.concatenate([reach, jnp.zeros_like(reach)], axis=1)
        left = left + jnp.where(diagonal, reach, 0.0)
        end_bound = jnp.sum(jnp.where(diagonal, sums[height:height + 1], 0.0), axis=1, keepdims=True)
        parts = [left] + [parts_ref[:size, at:at + lanes] for at in range(0, width, lanes)]
        own, other = jnp.zeros((size, lanes), F32), jnp.zeros((size, lanes), F32)
        for k in range(0, size, 2):
            first = jnp.broadcast_to(parts[0][:, k:k + 1], (size, lanes))
            second = jnp.broadcast_to(parts[0][:, k + 1:k + 2], (size, lanes))
            a, b, c, d = first[k:k + 1], second[k:k + 1], first[k + 1:k + 2], second[k + 1:k + 2]
            inverse = 1.0 / (a * d - b * c)
            upper, lower = rows == k, rows == k + 1
            pivots = upper | lower
            up = jnp.where(pivots, 0.0, (first * d - second * c) * inverse)
            down = jnp.where(pivots, 0.0, (second * a - first * b) * inverse)
            own = jnp.where(upper, d * inverse, jnp.where(lower, a * inverse, own))
            other = jnp.where(upper, -b * inverse, jnp.where(lower, -c * inverse, other))
            parts = [values - up * values[k:k + 1] - down * values[k + 1:k + 2] for values in parts]
        even = rows % 2 == 0
        for at, values in enumerate(parts[1:]):
            following = jnp.concatenate([values[1:], values[:1]], axis=0)
            previous = jnp.concatenate([values[-1:], values[:-1]], axis=0)
            solved = own * values + other * jnp.where(even, following, previous)
            here = slice(at * lanes, (at + 1) * lanes)
            out_ref[:, here] = solved * unit_of(end_bound)
            bound = parts_ref[size:size + 1, here] + jnp.sum(jnp.abs(solved) * end_bound, axis=0, keepdims=True)
            unit_ref[:, here] = unit_of(bound)

    out_shape = tuple(jax.ShapeDtypeStruct((height, width), F32) for height in (size, 1))
    params = pltpu.CompilerParams(vmem_limit_bytes=8 * 1024 * 1024)
    return pl.pallas_call(body, out_shape=out_shape, compiler_params=params)(mine, other, impedance, flags, parts)


def on_device(sensitivity, injections, from_node, to_node, switch_flags, impedance):
    row_count, col_count = sensitivity.shape
    row = lax.axis_index("row")
    col = lax.axis_index("col")
    y, core = row // (Z * CORES), row % CORES
    slots = injections.shape[1]

    loads = injections.T
    pair = lax.all_gather(loads, "row", axis_index_groups=ALONG_Y, axis=0)

    row_select = incidence_of(row * row_count + jnp.arange(row_count, dtype=jnp.int32), from_node, to_node)
    copies = differences(sensitivity, (jnp.stack([from_node, to_node]) - col * col_count).astype(F32))

    gathered = lax.all_gather(pair, "row", axis_index_groups=ALONG_Z_CORE, axis=0)

    parts = lax.all_to_all(copies, "col", 0, 0, tiled=True)
    parts = jnp.sum(parts, axis=0)
    columns_t, row_bound = parts[:BR], parts[BR:]

    half = row_count // 2
    first, second = columns_t[:, :half], columns_t[:, half:]
    cap_part = jnp.dot(columns_t, row_select, precision=HIGH, preferred_element_type=F32)
    cap_part = jnp.concatenate([cap_part[: BR // 2], cap_part[BR // 2:]], axis=1)
    end_bound = jnp.dot(row_bound, jnp.abs(row_select), precision=HIGH, preferred_element_type=F32)
    cap_part = jnp.concatenate([cap_part, jnp.concatenate([end_bound, end_bound], axis=1)], axis=0)
    give = jnp.concatenate([jnp.where(y == 0, second, first), cap_part], axis=0)
    take = lax.ppermute(give, "row", OTHER_Y)
    blocks = COLS // Y
    block = jnp.where(col // blocks == y, jnp.where(y == 0, first, second), take[:BR])
    line = lax.all_gather(
        jnp.concatenate([block, cap_part + take[BR:]], axis=0), "row", axis_index_groups=ALONG_Z, axis=0
    )
    zs = Z // blocks
    ends = lax.dynamic_slice_in_dim(line[:, :BR], (col % blocks) * zs, zs, 0).reshape(zs * BR, half)
    mine = jnp.concatenate([ends, jnp.sum(line[:, BR:], axis=0)], axis=0)
    other = lax.ppermute(mine, "row", OTHER_CORE)
    ends = in_order(core, mine[: zs * BR], other[: zs * BR])
    end_bound = mine[-8, :BR] + other[-8, :BR]
    ends = ends.reshape(CORES, zs, BR, half) * (1.0 / unit_of(end_bound))[:, None]
    other_ends = lax.ppermute(ends.astype(jnp.float16), "row", OTHER_Y)

    solved, unit = solve(mine, other, impedance[None], switch_flags[None], parts)

    loads = gathered.reshape(blocks, zs * CORES, Y, slots, col_count)
    packed, units = products(loads, sensitivity, solved, ends, other_ends.astype(F32), unit, y)

    arrived = lax.all_to_all(packed.astype(jnp.float16), "col", 0, 0, tiled=True)
    total = jnp.sum(arrived.astype(F32), axis=0) * units
    return total


def solution(mesh):
    placed = (P("row", "col"), P("col", "row"), P(), P(), P(), P())
    return jax.shard_map(
        on_device, mesh=mesh, in_specs=placed, out_specs=P("row", "col"), check_vma=False
    )
```
